512 devices in a mesh: seq: 32 (over x, z), tp: 8 (over y), dp: 2 (over core).
Axes of the slice: x: 4, y: 8, z: 8, core: 2. Of those that a mesh axis runs over, the one named last changes fastest.
Arguments:
- qkv_bank: bfloat16 [32768, 3, 4096], P(('dp', 'seq'), None, 'tp'), parts along dimension 0, may hold values from -6 to 6
- pack_rows: int32 [256], P(('dp', 'seq')), parts along dimension 0, may hold values from 0 to 127, as said below
- segment: int32 [256], P(('dp', 'seq')), parts along dimension 0, may hold values from 0 to 7, never falling along the last dimension, each value on 1 to 64 neighbouring positions
- norm_gain: float32 [4096], P('tp'), may hold values from 0.1 to 1.9
- out_weight: bfloat16 [4096, 4096], P('seq', 'tp'), may hold values from -0.09375 to 0.09375
Outputs:
- mixed: bfloat16 [32768, 4096], P(('dp', 'seq'), 'tp'), parts along dimension 0
The draws below stay inside these ranges and needn't reach their ends.
There are 2 independent parts, one for each index of `dp`. The reference program is written for one: setup_inputs(seed, part) draws one part's arguments, and reference() takes and returns one part's arrays. A program takes and returns all parts, laid end to end along the dimension named above; an argument that names none is the same for every part. Nothing has to cross between parts.
Inputs may be any that keep to these rules, and one draw needn't show every extreme that they name: Packed block t takes block pack_rows[t]; the 4 packed blocks of each aligned group of 4 take the same group's 4 source blocks in some order. Segment ids never fall along the packed blocks; a segment covers at most 64 blocks, and one covers exactly that many.
All inputs are finite; a program needn't handle non-finite values.
Results may differ from the reference program's by a relative error of at most 0.0057.
Values may be sent and summed in bfloat16 or wider, within the bound.
A program may use at most 64 MiB of HBM per device.

```python
import math
import jax
import jax.numpy as jnp
import numpy as np
from jax import lax

D = 4096
H = 32
DH = 128
BLK = 128
HD = 4096
TOKENS = 16384
NB = 128
BPD = 4


def draw_pack_rows(key, part):
    key = jax.random.fold_in(key, 11)
    groups = NB // BPD
    keys = jax.random.split(key, groups)
    orders = jax.vmap(lambda single: jax.random.permutation(single, BPD))(keys)
    base = jnp.arange(groups, dtype=jnp.int32)[:, None] * BPD
    return (orders.astype(jnp.int32) + base).reshape(NB).astype(jnp.int32)


def block_levels(own_key, shape, shards, least, largest):
    loudness, own = 1.0, jax.random.fold_in(own_key, 6)
    for dim, parts in shards:
        steps = jnp.exp(jax.random.uniform(jax.random.fold_in(own, dim), (parts,), jnp.float32, least / len(shards), largest / len(shards)))
        loudness = loudness * jnp.repeat(steps, shape[dim] // parts).reshape([-1 if axis == dim else 1 for axis in range(len(shape))])
    return loudness


def length_profile(amount, total, bound, skew):
    loads = [(1 << 20) // math.isqrt(grade ** skew) + 1 for grade in range(2, amount + 1)]
    rest, given = total - bound - (amount - 1), [1] * (amount - 1)
    while rest > 0:
        movable = [i for i in range(amount - 1) if given[i] < bound]
        pool, left = sum([loads[i] for i in movable]), rest
        for i in movable:
            addition = min(bound - given[i], max(1, left * loads[i] // pool), rest)
            given[i] = given[i] + addition
            rest = rest - addition
    return np.array([bound] + given)


def ragged(rng, amount, total, most, lean):
    if amount == 2:
        one = jax.random.randint(rng, (), max(1, total - most), min(most, total - 1) + 1)
        return jnp.stack([one, total - one])
    tallies = jnp.asarray(length_profile(amount, total, most, lean), jnp.int32)
    couples = (amount - 1) // 2
    source_of, receiver = tallies[1:1 + 2 * couples:2], tallies[2:2 + 2 * couples:2]
    slack = jnp.minimum(source_of - 1, most - receiver)
    moved = jax.random.randint(jax.random.fold_in(rng, 1), (couples,), 0, 1 << 20) % (slack + 1)
    tallies = tallies.at[1:1 + 2 * couples:2].set(source_of - moved).at[2:2 + 2 * couples:2].set(receiver + moved)
    return tallies[jax.random.permutation(jax.random.fold_in(rng, 2), amount)]


def noise(stream_key, shape, deviation, reach, shards=(), kind=jnp.bfloat16):
    gain = block_levels(stream_key, shape, shards, -0.22, 0.18) if shards else 1.0
    result = jax.random.normal(stream_key, shape, jnp.float32) * deviation * gain
    return jnp.minimum(jnp.maximum(result, -reach), reach).astype(kind)


def setup_inputs(seed: int = 0, part: int = 0) -> dict:
    splits = jax.random.split(jax.random.key(seed), 6)
    own_keys = jax.random.split(jax.random.fold_in(splits[5], part), 6)
    return {
        "qkv_bank": noise(own_keys[0], (TOKENS, 3, HD), 1.0, 6.0, ((0, 32), (2, 8))),
        "pack_rows": draw_pack_rows(jax.random.fold_in(jax.random.fold_in(splits[5], part), 71), part),
        "segment": jnp.searchsorted(jnp.cumsum(ragged(own_keys[2], 8, NB, NB // 2, 2)), jnp.arange(NB), side="right").astype(jnp.int32),
        "norm_gain": jnp.clip(1.0 + 0.18 * jax.random.normal(splits[3], (HD,), jnp.float32), 0.1, 1.9),
        "out_weight": noise(splits[4], (HD, D), HD ** -0.5, 0.09375, ((0, 32), (1, 8))),
    }


def reference(qkv_bank, pack_rows, segment, norm_gain, out_weight):
    blocks = qkv_bank.reshape(NB, BLK, 3, H, DH)
    packed = jnp.take(blocks, pack_rows.astype(jnp.int32), axis=0)
    gains = norm_gain.reshape(H, DH)
    causal = jnp.arange(BLK)[:, None] >= jnp.arange(BLK)[None, :]

    def advance(carry, inputs):
        state, previous = carry
        block, seg_now = inputs
        keep = (seg_now == previous).astype(jnp.float32)
        state = state * keep
        queries = block[:, 0].astype(jnp.float32)
        keys = block[:, 1].astype(jnp.float32)
        values = block[:, 2].astype(jnp.float32)
        prefix = lax.optimization_barrier(state.astype(jnp.bfloat16)).astype(jnp.float32)
        inter = jnp.einsum('ihd,hde->ihe', queries, prefix, precision=lax.Precision.HIGHEST)
        scores = jnp.einsum('ihd,jhd->hij', queries, keys, precision=lax.Precision.HIGHEST)
        scores = jnp.where(causal[None], scores, 0.0)
        scores = lax.optimization_barrier(scores.astype(jnp.bfloat16)).astype(jnp.float32)
        intra = jnp.einsum('hij,jhe->ihe', scores, values, precision=lax.Precision.HIGHEST)
        attended = inter + intra
        scale = lax.rsqrt(lax.optimization_barrier(jnp.mean(attended * attended, axis=-1, keepdims=True)) + 1e-06)
        normed = (attended * scale * gains[None]).astype(jnp.bfloat16)
        state = state + jnp.einsum('jhd,jhe->hde', keys, values, precision=lax.Precision.HIGHEST)
        return ((state, seg_now), normed)
    start = (jnp.zeros((H, DH, DH), jnp.float32), jnp.array(-1, jnp.int32))
    carry_out, normed = lax.scan(advance, start, (packed, segment.astype(jnp.int32)))
    normed = normed.reshape(TOKENS, HD)
    return jnp.dot(normed, out_weight, preferred_element_type=jnp.float32).astype(jnp.bfloat16)
```

```python
import jax
import jax.numpy as jnp
from jax import lax
from jax.experimental import pallas as pl
from jax.experimental.pallas import tpu as pltpu
from jax.sharding import PartitionSpec as P

DH = 128
BLK = 128
NB = 4
NH = 4
NX, NZ, NY = 4, 8, 8
PIECE = NH * DH // NZ
W0 = 48
MESH = pl.DeviceIdType.MESH
F32, BF16 = jnp.float32, jnp.bfloat16


def dot(a, b, dims=(((1,), (0,)), ((), ()))):
    return lax.dot_general(a, b, dims, preferred_element_type=F32)


def same(a, b):
    return jnp.maximum(1 - jnp.abs(a - b), 0).astype(F32)


def hops(direction, block):
    return 4 if (block < NB // 2) == (direction == 0) else 3


def kernel(
    pack_ref, seg_ref, qkv_hbm, gain_ref, w_hbm, out_ref,
    qbuf, kbuf, vbuf, wbuf, feats, acc, intra, local, tsend, pieces, infos, ascan, rbuf, csend, carry,
    load_sem, info_s, info_r, t_s, t_r, r_s, r_r, c_s, c_r,
    y_s, y_r, wx_s, wx_r, wz_s, wz_r, pair_s, pair_r,
):
    seq, tp, core = lax.axis_index("seq"), lax.axis_index("tp"), lax.axis_index("dp")
    x, z = seq // NZ, seq % NZ

    def at_z(step):
        return {"seq": x * NZ + (z + step) % NZ, "tp": tp, "dp": core}

    def at_x(step):
        return {"seq": (x + step) % NX * NZ + z, "tp": tp, "dp": core}

    def at_y(step):
        return {"seq": seq, "tp": (tp + step) % NY, "dp": core}

    sibling = {"seq": seq, "tp": tp, "dp": 1 - core}

    def remote(src, dst, send, recv, device):
        return pltpu.make_async_remote_copy(
            src_ref=src, dst_ref=dst, send_sem=send, recv_sem=recv,
            device_id=device, device_id_type=MESH,
        )

    loads = [pltpu.make_async_copy(qkv_hbm.at[p], to, load_sem.at[p]) for p, to in enumerate((qbuf, kbuf, vbuf))]
    rows_of = (pl.ds(0, W0), pl.ds(W0, BLK - W0))
    w_load = [
        pltpu.make_async_copy(w_hbm.at[rows], wbuf.at[x, z, rows], load_sem.at[3]) for rows in rows_of
    ]

    for p in (1, 2, 0):
        loads[p].start()
    for c in range(2):
        pl.when(core == c)(w_load[c].start)
    partners = [at_z(i) for i in range(1, NZ)] + [at_x(i) for i in range(1, NX)]
    partners += [at_y(1), at_y(NY - 1), sibling]
    barrier = pltpu.get_barrier_semaphore()
    for device in partners:
        pl.semaphore_signal(barrier, inc=1, device_id=device, device_id_type=MESH)
    segs = [seg_ref[b] for b in range(NB)]
    infos[z, 0:4, :] = jnp.broadcast_to(segs[0], (4, DH)).astype(F32)
    infos[z, 4:8, :] = jnp.broadcast_to(segs[NB - 1], (4, DH)).astype(F32)
    pl.semaphore_wait(barrier, len(partners))

    info_copies = [
        remote(infos.at[z], infos.at[z], info_s.at[i - 1], info_r.at[i - 1], at_z(i))
        for i in range(1, NZ)
    ]
    for copy in info_copies:
        copy.start()

    w_x0 = [
        remote(wbuf.at[x, z, rows_of[0]], wbuf.at[x, z, rows_of[0]], wx_s.at[i - 1], wx_r.at[i - 1], at_x(i))
        for i in range(1, NX)
    ]
    w_z0 = [
        remote(wbuf.at[:, z, rows_of[0]], wbuf.at[:, z, rows_of[0]], wz_s.at[i - 1], wz_r.at[i - 1], at_z(i))
        for i in range(1, NZ)
    ]
    w_z1 = [
        remote(wbuf.at[x, z, rows_of[1]], wbuf.at[x, z, rows_of[1]], wz_s.at[i - 1], wz_r.at[i - 1], at_z(i))
        for i in range(1, NZ)
    ]
    w_x1 = [
        remote(wbuf.at[x, :, rows_of[1]], wbuf.at[x, :, rows_of[1]], wx_s.at[i - 1], wx_r.at[i - 1], at_x(i))
        for i in range(1, NX)
    ]

    @pl.when(core == 0)
    def _():
        w_load[0].wait()
        for copy in w_x0:
            copy.start()

    @pl.when(core == 1)
    def _():
        w_load[1].wait()

    ids = [lax.rem(pack_ref[b], NB) for b in range(NB)]
    heads = [pl.ds(h * DH, DH) for h in range(NH)]
    joins = [None] + [same(segs[b], segs[b - 1]) for b in range(1, NB)]
    loads[1].wait()
    loads[2].wait()
    for h in range(NH):
        total = None
        for b in range(NB):
            key = kbuf[ids[b], :, heads[h]]
            value = vbuf[ids[b], :, heads[h]]
            update = dot(key, value, (((0,), (0,)), ((), ())))
            if b > 0:
                before = total * joins[b]
                local[b - 1, h] = before
                total = before + update
            else:
                total = update
        tsend[pl.ds(h * DH, DH), :] = total.astype(BF16)

    def piece(j):
        return pl.ds(pl.multiple_of(j * PIECE, PIECE), PIECE)

    t_copies = [
        remote(tsend.at[piece((z + i) % NZ)], pieces.at[z], t_s.at[i - 1], t_r.at[i - 1], at_z(i))
        for i in range(1, NZ)
    ]
    for copy in t_copies:
        copy.start()
    pieces[z] = tsend[piece(z), :]

    loads[0].wait()
    causal = lax.broadcasted_iota(jnp.int32, (BLK, BLK), 0) >= lax.broadcasted_iota(jnp.int32, (BLK, BLK), 1)

    def block_rows(b):
        return pl.ds(b * BLK, BLK)

    for b in range(NB):
        for h in range(NH):
            query = qbuf[ids[b], :, heads[h]]
            key = kbuf[ids[b], :, heads[h]]
            value = vbuf[ids[b], :, heads[h]]
            score = dot(query, key, (((1,), (1,)), ((), ())))
            score = jnp.where(causal, score, 0.0).astype(BF16)
            intra[block_rows(b), heads[h]] = dot(score, value)

    for copy in info_copies:
        copy.wait_recv()
    for copy in t_copies:
        copy.wait_recv()
    firsts = [infos[j, 0:1, :] for j in range(NZ)]
    lasts = [infos[j, 4:5, :] for j in range(NZ)]
    running = None
    for j in range(NZ):
        part = pieces[j].astype(F32)
        if j > 0:
            before = same(firsts[j], lasts[j - 1]) * running
            ascan[j] = before
            running = part + same(firsts[j], lasts[j]) * before
        else:
            running = part
    rbuf[x, 0:PIECE, :] = running
    rbuf[x, PIECE:PIECE + 8, :] = jnp.broadcast_to(lasts[NZ - 1], (8, DH))
    r_copies = [
        remote(rbuf.at[x], rbuf.at[x], r_s.at[i - 1], r_r.at[i - 1], at_x(i)) for i in range(1, NX)
    ]
    for copy in r_copies:
        copy.start()
    for copy in r_copies:
        copy.wait_recv()
    for j in range(NZ):
        into = ascan[j] if j > 0 else jnp.zeros((PIECE, DH), F32)
        for xx in range(NX - 1):
            hit = same(rbuf[xx, PIECE:PIECE + 1, :], firsts[j]) * jnp.where(xx < x, 1.0, 0.0)
            into = into + hit * rbuf[xx, 0:PIECE, :]
        csend[j] = into.astype(BF16)
    c_copies = [
        remote(csend.at[(z + i) % NZ], carry.at[z], c_s.at[i - 1], c_r.at[i - 1], at_z(i))
        for i in range(1, NZ)
    ]
    for copy in c_copies:
        copy.start()
    carry[z] = csend[z]

    @pl.when(core == 0)
    def _():
        for copy in w_x0:
            copy.wait_recv()
        for copy in w_z0:
            copy.start()

    @pl.when(core == 1)
    def _():
        for copy in w_z1:
            copy.start()

    for copy in c_copies:
        copy.wait_recv()

    def y_copy(direction, step, b):
        source = (tp - step) % NY if direction == 0 else (tp + step) % NY
        ref = feats.at[source, block_rows(b)]
        to = at_y(1) if direction == 0 else at_y(NY - 1)
        return remote(ref, ref, y_s.at[direction, step, b], y_r.at[direction, step, b], to)

    gains = gain_ref[...]
    for b in range(NB):
        carried = same(segs[b], segs[0])
        for h in range(NH):
            state = carry[pl.ds(h * 2, 2)].reshape(DH, DH).astype(F32) * carried
            if b > 0:
                state = state + local[b - 1, h]
            query = qbuf[ids[b], :, heads[h]]
            attended = intra[block_rows(b), heads[h]] + dot(query, state.astype(BF16))
            scale = lax.rsqrt(jnp.mean(attended * attended, axis=-1, keepdims=True) + 1e-06)
            normed = attended * scale * gains[:, h * DH:(h + 1) * DH]
            feats[tp, block_rows(b), heads[h]] = normed.astype(BF16)
        for direction in range(2):
            y_copy(direction, 0, b).start()

    def arrive(step, b):
        for direction in range(2):
            if hops(direction, b) > step:
                y_copy(direction, step, b).wait_recv()
                if hops(direction, b) > step + 1:
                    y_copy(direction, step + 1, b).start()

    for b in range(NB - 1):
        arrive(0, b)

    @pl.when(core == 1)
    def _():
        for copy in w_z1:
            copy.wait_recv()
        for copy in w_x1:
            copy.start()

    arrive(0, NB - 1)
    for b in range(NB):
        arrive(1, b)

    pair = [remote(wbuf.at[:, :, rows], wbuf.at[:, :, rows], pair_s, pair_r, sibling) for rows in rows_of]

    @pl.when(core == 0)
    def _():
        for copy in w_z0:
            copy.wait_recv()
        pair[0].start()

    @pl.when(core == 1)
    def _():
        for copy in w_x1:
            copy.wait_recv()
        pair[1].start()

    for b in range(NB):
        arrive(2, b)
    for c in range(2):
        pl.when(core == c)(pair[1 - c].wait_recv)

    def weights(source):
        return wbuf[source // 2, pl.ds(source % 2 * NH, NH)].reshape(NH * DH, NH * DH)

    acc[...] = dot(feats[tp], weights(tp))

    def product(i, _):
        source = (tp + jnp.where(i < 3, i + 1, i + 2)) % NY
        acc[...] += dot(feats[source], weights(source))
        return 0

    lax.fori_loop(0, NY - 2, product, 0)

    far = (tp + NY // 2) % NY
    for b in (0, NB // 2, 1, NB // 2 + 1):
        arrive(3, b)
        mixed = acc[block_rows(b), :] + dot(feats[far, block_rows(b), :], weights(far))
        out_ref[block_rows(b), :] = mixed.astype(BF16)

    for copy in info_copies + t_copies + r_copies + c_copies:
        copy.wait_send()
    for direction in range(2):
        for b in range(NB):
            for step in range(hops(direction, b)):
                y_copy(direction, step, b).wait_send()

    @pl.when(core == 0)
    def _():
        for copy in w_x0 + w_z0:
            copy.wait_send()
        pair[0].wait_send()

    @pl.when(core == 1)
    def _():
        for copy in w_z1 + w_x1:
            copy.wait_send()
        pair[1].wait_send()


def body(qkv_bank, pack_rows, segment, norm_gain, out_weight):
    rows, _, columns = qkv_bank.shape
    planes = jnp.transpose(qkv_bank, (1, 0, 2)).reshape(3, NB, BLK, columns)
    dma = pltpu.SemaphoreType.DMA
    return pl.pallas_call(
        kernel,
        out_shape=jax.ShapeDtypeStruct((rows, columns), BF16),
        in_specs=[
            pl.BlockSpec(memory_space=pltpu.SMEM),
            pl.BlockSpec(memory_space=pltpu.SMEM),
            pl.BlockSpec(memory_space=pl.ANY),
            pl.BlockSpec(memory_space=pltpu.VMEM),
            pl.BlockSpec(memory_space=pl.ANY),
        ],
        out_specs=pl.BlockSpec(memory_space=pltpu.VMEM),
        scratch_shapes=[
            pltpu.VMEM((NB, BLK, columns), BF16),
            pltpu.VMEM((NB, BLK, columns), BF16),
            pltpu.VMEM((NB, BLK, columns), BF16),
            pltpu.VMEM((NX, NZ, BLK, columns), BF16),
            pltpu.VMEM((NY, rows, columns), BF16),
            pltpu.VMEM((rows, columns), F32),
            pltpu.VMEM((rows, columns), F32),
            pltpu.VMEM((NB - 1, NH, DH, DH), F32),
            pltpu.VMEM((NH * DH, DH), BF16),
            pltpu.VMEM((NZ, PIECE, DH), BF16),
            pltpu.VMEM((NZ, 8, DH), F32),
            pltpu.VMEM((NZ, PIECE, DH), F32),
            pltpu.VMEM((NX, PIECE + 8, DH), F32),
            pltpu.VMEM((NZ, PIECE, DH), BF16),
            pltpu.VMEM((NZ, PIECE, DH), BF16),
            dma((4,)),
            dma((NZ - 1,)), dma((NZ - 1,)), dma((NZ - 1,)), dma((NZ - 1,)),
            dma((NX - 1,)), dma((NX - 1,)), dma((NZ - 1,)), dma((NZ - 1,)),
            dma((2, 4, NB)), dma((2, 4, NB)),
            dma((NX - 1,)), dma((NX - 1,)), dma((NZ - 1,)), dma((NZ - 1,)),
            dma, dma,
        ],
        compiler_params=pltpu.CompilerParams(
            collective_id=0, has_side_effects=True, vmem_limit_bytes=48 * 1024 * 1024
        ),
    )(pack_rows, segment, planes, norm_gain.reshape(1, columns), out_weight)


def solution(mesh):
    in_specs = (
        P(("dp", "seq"), None, "tp"),
        P(("dp", "seq")),
        P(("dp", "seq")),
        P("tp"),
        P("seq", "tp"),
    )
    out_specs = P(("dp", "seq"), "tp")
    return jax.shard_map(body, mesh=mesh, in_specs=in_specs, out_specs=out_specs, check_vma=False)
```

```python
import jax
import jax.numpy as jnp
from jax import lax
from jax.experimental import pallas as pl
from jax.experimental.pallas import tpu as pltpu
from jax.sharding import PartitionSpec as P

DH = 128
BLK = 128
NB = 4
NH = 4
NG = 2
GH = NH // NG
GC = GH * DH
NX, NZ, NY = 4, 8, 8
PIECE = GC // NZ
HALF = BLK // 2
MESH = pl.DeviceIdType.MESH
F32, BF16 = jnp.float32, jnp.bfloat16


def dot(a, b, dims=(((1,), (0,)), ((), ()))):
    return lax.dot_general(a, b, dims, preferred_element_type=F32)


def same(a, b):
    return jnp.maximum(1 - jnp.abs(a - b), 0).astype(F32)


def hops(direction, part):
    return 4 if (part < 2) == (direction == 0) else 3


def kernel(
    pack_ref, seg_ref, qkv_hbm, gain_ref, w_hbm, out_hbm,
    qbuf, kbuf, vbuf, wbuf, feats, acc, intra, local, tsend, pieces, infos, ascan, rbuf, csend, carry, mixed,
    load_sem, out_sem, info_s, info_r, t_s, t_r, r_s, r_r, c_s, c_r,
    y_s, y_r, wx_s, wx_r, wz_s, wz_r, own_s, own_r, pair_s, pair_r,
):
    seq, tp, core = lax.axis_index("seq"), lax.axis_index("tp"), lax.axis_index("dp")
    x, z = seq // NZ, seq % NZ

    def at_z(step):
        return {"seq": x * NZ + (z + step) % NZ, "tp": tp, "dp": core}

    def at_x(step):
        return {"seq": (x + step) % NX * NZ + z, "tp": tp, "dp": core}

    def at_y(step):
        return {"seq": seq, "tp": (tp + step) % NY, "dp": core}

    sibling = {"seq": seq, "tp": tp, "dp": 1 - core}

    def remote(src, dst, send, recv, device):
        return pltpu.make_async_remote_copy(
            src_ref=src, dst_ref=dst, send_sem=send, recv_sem=recv,
            device_id=device, device_id_type=MESH,
        )

    loads = [
        pltpu.make_async_copy(qkv_hbm.at[p], to, load_sem.at[p]) for p, to in enumerate((qbuf, kbuf, vbuf))
    ]
    w_load = pltpu.make_async_copy(w_hbm.at[core], wbuf.at[x, z, core], load_sem.at[3])
    loads[1].start()
    loads[2].start()
    partners = [at_z(i) for i in (4, 3, 5, 2, 6, 1, 7)] + [at_x(i) for i in (2, 1, 3)]
    partners += [at_y(1), at_y(NY - 1), sibling]
    barrier = pltpu.get_barrier_semaphore()
    for device in partners:
        pl.semaphore_signal(barrier, inc=1, device_id=device, device_id_type=MESH)
    loads[0].start()
    w_load.start()
    segs = [seg_ref[b] for b in range(NB)]
    infos[z, 0:4, :] = jnp.broadcast_to(segs[0], (4, DH)).astype(F32)
    infos[z, 4:8, :] = jnp.broadcast_to(segs[NB - 1], (4, DH)).astype(F32)

    ids = [lax.rem(pack_ref[b], NB) for b in range(NB)]
    heads = [pl.ds(h * DH, DH) for h in range(NH)]
    joins = [None] + [same(segs[b], segs[b - 1]) for b in range(1, NB)]

    def update(g):
        for h in range(GH):
            head = g * GH + h
            total = None
            for b in range(NB):
                key = kbuf[ids[b], :, heads[head]]
                value = vbuf[ids[b], :, heads[head]]
                new = dot(key, value, (((0,), (0,)), ((), ())))
                if b > 0:
                    before = total * joins[b]
                    local[b - 1, head] = before
                    total = before + new
                else:
                    total = new
            tsend[g, pl.ds(h * DH, DH), :] = total.astype(BF16)
        pieces[g, z] = tsend[g, piece(z), :]

    def piece(j):
        return pl.ds(pl.multiple_of(j * PIECE, PIECE), PIECE)

    far_first = (4, 3, 5, 2, 6, 1, 7)
    info_copies = [
        remote(infos.at[z], infos.at[z], info_s.at[i - 1], info_r.at[i - 1], at_z(i)) for i in far_first
    ]
    t_copies = [
        [
            remote(tsend.at[g, piece((z + i) % NZ)], pieces.at[g, z], t_s.at[g, i - 1], t_r.at[g, i - 1], at_z(i))
            for i in far_first
        ]
        for g in range(NG)
    ]
    w_x = [
        remote(wbuf.at[x, z, core], wbuf.at[x, z, core], wx_s.at[i - 1], wx_r.at[i - 1], at_x(i)) for i in (2, 1, 3)
    ]
    loads[1].wait()
    loads[2].wait()
    update(0)
    pl.semaphore_wait(barrier, len(partners))
    for copy in t_copies[0] + info_copies:
        copy.start()
    update(1)
    for copy in t_copies[1]:
        copy.start()
    w_load.wait()
    for copy in w_x:
        copy.start()

    loads[0].wait()
    causal = lax.broadcasted_iota(jnp.int32, (BLK, BLK), 0) >= lax.broadcasted_iota(jnp.int32, (BLK, BLK), 1)

    def block_rows(b):
        return pl.ds(b * BLK, BLK)

    for h in range(NH):
        for b in range(NB):
            query = qbuf[ids[b], :, heads[h]]
            key = kbuf[ids[b], :, heads[h]]
            value = vbuf[ids[b], :, heads[h]]
            score = dot(query, key, (((1,), (1,)), ((), ())))
            score = jnp.where(causal, score, 0.0).astype(BF16)
            intra[block_rows(b), heads[h]] = dot(score, value)

    for copy in info_copies:
        copy.wait_recv()
    firsts = [infos[j, 0:1, :] for j in range(NZ)]
    lasts = [infos[j, 4:5, :] for j in range(NZ)]
    stays = [same(firsts[j], lasts[j]) for j in range(NZ)]
    follows = [None] + [same(firsts[j], lasts[j - 1]) for j in range(1, NZ)]
    r_copies = [
        [remote(rbuf.at[g, x], rbuf.at[g, x], r_s.at[g, i - 1], r_r.at[g, i - 1], at_x(i)) for i in (2, 1, 3)]
        for g in range(NG)
    ]
    c_copies = [
        [
            remote(csend.at[g, (z + i) % NZ], carry.at[g, z], c_s.at[g, i - 1], c_r.at[g, i - 1], at_z(i))
            for i in far_first
        ]
        for g in range(NG)
    ]
    for g in range(NG):
        for copy in t_copies[g]:
            copy.wait_recv()
        running = pieces[g, 0].astype(F32)
        for j in range(1, NZ):
            before = follows[j] * running
            ascan[g, j] = before
            running = pieces[g, j].astype(F32) + stays[j] * before
        rbuf[g, x, 0:PIECE, :] = running
        rbuf[g, x, PIECE:PIECE + 8, :] = jnp.broadcast_to(lasts[NZ - 1], (8, DH))
        for copy in r_copies[g]:
            copy.start()
    for g in range(NG):
        for copy in r_copies[g]:
            copy.wait_recv()
        for j in range(NZ):
            into = ascan[g, j] if j > 0 else jnp.zeros((PIECE, DH), F32)
            for xx in range(NX - 1):
                hit = same(rbuf[g, xx, PIECE:PIECE + 1, :], firsts[j]) * jnp.where(xx < x, 1.0, 0.0)
                into = into + hit * rbuf[g, xx, 0:PIECE, :]
            csend[g, j] = into.astype(BF16)
        for copy in c_copies[g]:
            copy.start()
        carry[g, z] = csend[g, z]

    def w_copy(direction, step, j):
        source = (z - step) % NZ if direction == 0 else (z + step) % NZ
        ref = wbuf.at[j, source, core]
        to = at_z(1) if direction == 0 else at_z(NZ - 1)
        return remote(ref, ref, wz_s.at[direction, step, j], wz_r.at[direction, step, j], to)

    def w_pair(direction, step, j):
        source = (z - 1 - step) % NZ if direction == 0 else (z + 1 + step) % NZ
        ref = wbuf.at[j, source, core]
        return remote(ref, ref, pair_s.at[direction, step, j], pair_r.at[direction, step, j], sibling)

    own_pair = remote(wbuf.at[:, z, core], wbuf.at[:, z, core], own_s, own_r, sibling)
    for copy in w_x:
        copy.wait_recv()
    for j in range(NX):
        for direction in range(2):
            w_copy(direction, 0, j).start()
    own_pair.start()

    def w_arrive(step, j):
        for direction in range(2):
            if hops(direction, j) > step:
                w_copy(direction, step, j).wait_recv()
                if hops(direction, j) > step + 1:
                    w_copy(direction, step + 1, j).start()
                w_pair(direction, step, j).start()

    def y_copy(direction, step, g, b):
        source = (tp - step) % NY if direction == 0 else (tp + step) % NY
        ref = feats.at[source, g, block_rows(b)]
        to = at_y(1) if direction == 0 else at_y(NY - 1)
        return remote(ref, ref, y_s.at[direction, step, g, b], y_r.at[direction, step, g, b], to)

    def y_arrive(step, g, b):
        for direction in range(2):
            if hops(direction, b) > step:
                y_copy(direction, step, g, b).wait_recv()
                if hops(direction, b) > step + 1:
                    y_copy(direction, step + 1, g, b).start()

    gains = gain_ref[...]
    for g in range(NG):
        for copy in c_copies[g]:
            copy.wait_recv()
        for b in range(NB):
            carried = same(segs[b], segs[0])
            for h in range(GH):
                head = g * GH + h
                state = carry[g, pl.ds(h * NZ // GH, NZ // GH)].reshape(DH, DH).astype(F32) * carried
                if b > 0:
                    state = state + local[b - 1, head]
                query = qbuf[ids[b], :, heads[head]]
                attended = intra[block_rows(b), heads[head]] + dot(query, state.astype(BF16))
                scale = lax.rsqrt(jnp.mean(attended * attended, axis=-1, keepdims=True) + 1e-06)
                normed = attended * scale * gains[:, head * DH:(head + 1) * DH]
                feats[tp, g, block_rows(b), heads[h]] = normed.astype(BF16)
            for direction in range(2):
                y_copy(direction, 0, g, b).start()

    def weights(source, g):
        return wbuf[source // 2, pl.ds(source % 2 * NH + g * GH, GH)].reshape(GC, NH * DH)

    def product(step):
        source = (tp + step) % NY
        total = dot(feats[source, 0], weights(source, 0)) + dot(feats[source, 1], weights(source, 1))
        acc[...] = total if step == 0 else acc[...] + total

    parts = [(g, b) for g in range(NG) for b in range(NB)]
    w_order = [(step, j) for step in range(4) for j in range(NX)]
    for step in range(2):
        for i, (g, b) in enumerate(parts):
            y_arrive(step, g, b)
            w_arrive(*w_order[step * len(parts) + i])
    own_pair.wait_recv()
    for step, j in w_order:
        for direction in range(2):
            if hops(direction, j) > step:
                w_pair(direction, step, j).wait_recv()
    for i, (g, b) in enumerate(parts):
        y_arrive(2, g, b)
        if i < 5:
            product((0, 1, NY - 1, 2, NY - 2)[i])
    product(3)
    product(NY - 3)

    far = (tp + NY // 2) % NY
    out_copies = []
    for b in (0, NB // 2, 1, NB // 2 + 1):
        y_arrive(3, 0, b)
        y_arrive(3, 1, b)
        rows = block_rows(b)
        last = dot(feats[far, 0, rows, :], weights(far, 0)) + dot(feats[far, 1, rows, :], weights(far, 1))
        mixed[rows, :] = (acc[rows, :] + last).astype(BF16)
        out_copies.append(pltpu.make_async_copy(mixed.at[rows], out_hbm.at[rows], out_sem.at[b]))
        out_copies[-1].start()

    for copy in info_copies + w_x + [own_pair]:
        copy.wait_send()
    for g in range(NG):
        for copy in t_copies[g] + r_copies[g] + c_copies[g]:
            copy.wait_send()
    for direction in range(2):
        for part in range(4):
            for step in range(hops(direction, part)):
                w_copy(direction, step, part).wait_send()
                w_pair(direction, step, part).wait_send()
                for g in range(NG):
                    y_copy(direction, step, g, part).wait_send()
    for copy in out_copies:
        copy.wait()


def body(qkv_bank, pack_rows, segment, norm_gain, out_weight):
    rows, _, columns = qkv_bank.shape
    planes = jnp.transpose(qkv_bank, (1, 0, 2)).reshape(3, NB, BLK, columns)
    dma = pltpu.SemaphoreType.DMA
    return pl.pallas_call(
        kernel,
        out_shape=jax.ShapeDtypeStruct((rows, columns), BF16),
        in_specs=[
            pl.BlockSpec(memory_space=pltpu.SMEM),
            pl.BlockSpec(memory_space=pltpu.SMEM),
            pl.BlockSpec(memory_space=pl.ANY),
            pl.BlockSpec(memory_space=pltpu.VMEM),
            pl.BlockSpec(memory_space=pl.ANY),
        ],
        out_specs=pl.BlockSpec(memory_space=pl.ANY),
        scratch_shapes=[
            pltpu.VMEM((NB, BLK, columns), BF16),
            pltpu.VMEM((NB, BLK, columns), BF16),
            pltpu.VMEM((NB, BLK, columns), BF16),
            pltpu.VMEM((NX, NZ, 2, HALF, columns), BF16),
            pltpu.VMEM((NY, NG, rows, GC), BF16),
            pltpu.VMEM((rows, columns), F32),
            pltpu.VMEM((rows, columns), F32),
            pltpu.VMEM((NB - 1, NH, DH, DH), F32),
            pltpu.VMEM((NG, GC, DH), BF16),
            pltpu.VMEM((NG, NZ, PIECE, DH), BF16),
            pltpu.VMEM((NZ, 8, DH), F32),
            pltpu.VMEM((NG, NZ, PIECE, DH), F32),
            pltpu.VMEM((NG, NX, PIECE + 8, DH), F32),
            pltpu.VMEM((NG, NZ, PIECE, DH), BF16),
            pltpu.VMEM((NG, NZ, PIECE, DH), BF16),
            pltpu.VMEM((rows, columns), BF16),
            dma((4,)), dma((NB,)),
            dma((NZ - 1,)), dma((NZ - 1,)), dma((NG, NZ - 1)), dma((NG, NZ - 1)),
            dma((NG, NX - 1)), dma((NG, NX - 1)), dma((NG, NZ - 1)), dma((NG, NZ - 1)),
            dma((2, 4, NG, NB)), dma((2, 4, NG, NB)),
            dma((NX - 1,)), dma((NX - 1,)), dma((2, 4, NX)), dma((2, 4, NX)),
            dma, dma, dma((2, 4, NX)), dma((2, 4, NX)),
        ],
        compiler_params=pltpu.CompilerParams(
            collective_id=0, has_side_effects=True, vmem_limit_bytes=60 * 1024 * 1024
        ),
    )(pack_rows, segment, planes, norm_gain.reshape(1, columns), out_weight.reshape(2, HALF, columns))


def solution(mesh):
    in_specs = (
        P(("dp", "seq"), None, "tp"),
        P(("dp", "seq")),
        P(("dp", "seq")),
        P("tp"),
        P("seq", "tp"),
    )
    out_specs = P(("dp", "seq"), "tp")
    return jax.shard_map(body, mesh=mesh, in_specs=in_specs, out_specs=out_specs, check_vma=False)
```

```python
import jax
import jax.numpy as jnp
from jax import lax
from jax.experimental import pallas as pl
from jax.experimental.pallas import tpu as pltpu
from jax.sharding import PartitionSpec as P

DH = 128
BLK = 128
NB = 4
NH = 4
NG = 2
GH = NH // NG
GC = GH * DH
NX, NZ, NY = 4, 8, 8
PIECE = GC // NZ
HALF = BLK // 2
MESH = pl.DeviceIdType.MESH
F32, BF16 = jnp.float32, jnp.bfloat16


def dot(a, b, dims=(((1,), (0,)), ((), ()))):
    return lax.dot_general(a, b, dims, preferred_element_type=F32)


def same(a, b):
    return jnp.maximum(1 - jnp.abs(a - b), 0).astype(F32)


def hops(direction, part):
    return 4 if (part < 2) == (direction == 0) else 3


def kernel(
    pack_hbm, seg_hbm, qkv_hbm, gain_hbm, w_hbm, out_ref,
    pack_ref, seg_ref, gain_ref, qbuf, kbuf, vbuf, wbuf, feats, acc, intra, local, tsend, pieces, infos, ascan, rbuf,
    csend, carry,
    load_sem, info_s, info_r, t_s, t_r, r_s, r_r, c_s, c_r,
    y_s, y_r, wx_s, wx_r, wz_s, wz_r, pair_s, pair_r,
):
    seq, tp, core = lax.axis_index("seq"), lax.axis_index("tp"), lax.axis_index("dp")
    x, z = seq // NZ, seq % NZ

    def at_z(step):
        return {"seq": x * NZ + (z + step) % NZ, "tp": tp, "dp": core}

    def at_x(step):
        return {"seq": (x + step) % NX * NZ + z, "tp": tp, "dp": core}

    def at_y(step):
        return {"seq": seq, "tp": (tp + step) % NY, "dp": core}

    sibling = {"seq": seq, "tp": tp, "dp": 1 - core}

    def remote(src, dst, send, recv, device):
        return pltpu.make_async_remote_copy(
            src_ref=src, dst_ref=dst, send_sem=send, recv_sem=recv,
            device_id=device, device_id_type=MESH,
        )

    def wait_all(ref, sem):
        pltpu.make_async_copy(ref, ref, sem).wait()

    loads = [
        pltpu.make_async_copy(src, dst, load_sem.at[i])
        for i, (src, dst) in enumerate((
            (qkv_hbm.at[0], qbuf), (qkv_hbm.at[1], kbuf), (qkv_hbm.at[2], vbuf), (w_hbm.at[core], wbuf.at[x, z, core]),
            (pack_hbm, pack_ref), (seg_hbm, seg_ref), (gain_hbm, gain_ref),
        ))
    ]
    for i in (5, 4, 1, 2, 0, 3, 6):
        loads[i].start()
    partners = [at_z(i) for i in (4, 3, 5, 2, 6, 1, 7)] + [at_x(i) for i in (2, 1, 3)]
    partners += [at_y(1), at_y(NY - 1), sibling]
    barrier = pltpu.get_barrier_semaphore()
    for device in partners:
        pl.semaphore_signal(barrier, inc=1, device_id=device, device_id_type=MESH)
    loads[5].wait()
    loads[4].wait()
    segs = [seg_ref[b] for b in range(NB)]
    infos[z, 0:1, :] = jnp.broadcast_to(segs[0], (1, DH)).astype(F32)
    infos[z, 1:2, :] = jnp.broadcast_to(segs[NB - 1], (1, DH)).astype(F32)

    ids = [lax.rem(pack_ref[b], NB) for b in range(NB)]
    heads = [pl.ds(h * DH, DH) for h in range(NH)]
    joins = [None] + [same(segs[b], segs[b - 1]) for b in range(1, NB)]

    def update(g):
        for h in range(GH):
            head = g * GH + h
            total = None
            for b in range(NB):
                key = kbuf[ids[b], :, heads[head]]
                value = vbuf[ids[b], :, heads[head]]
                new = dot(key, value, (((0,), (0,)), ((), ())))
                if b > 0:
                    before = total * joins[b]
                    local[b - 1, head] = before
                    total = before + new
                else:
                    total = new
            tsend[g, pl.ds(h * DH, DH), :] = total.astype(BF16)
        pieces[g, z] = tsend[g, piece(z), :]

    def piece(j):
        return pl.ds(pl.multiple_of(j * PIECE, PIECE), PIECE)

    far_first = (4, 3, 5, 2, 6, 1, 7)
    def send_tails(g):
        for i in far_first:
            remote(tsend.at[g, piece((z + i) % NZ)], pieces.at[g, z], t_s, t_r.at[g], at_z(i)).start()

    loads[1].wait()
    loads[2].wait()
    update(0)
    pl.semaphore_wait(barrier, len(partners))
    send_tails(0)
    for i in far_first:
        remote(infos.at[z], infos.at[z], info_s, info_r, at_z(i)).start()
    update(1)
    send_tails(1)
    loads[3].wait()
    for i in (2, 1, 3):
        remote(wbuf.at[x, z, core], wbuf.at[x, z, core], wx_s, wx_r, at_x(i)).start()

    loads[0].wait()
    causal = lax.broadcasted_iota(jnp.int32, (BLK, BLK), 0) >= lax.broadcasted_iota(jnp.int32, (BLK, BLK), 1)

    def block_rows(b):
        return pl.ds(b * BLK, BLK)

    for h in range(NH):
        for b in range(NB):
            query = qbuf[ids[b], :, heads[h]]
            key = kbuf[ids[b], :, heads[h]]
            value = vbuf[ids[b], :, heads[h]]
            score = dot(query, key, (((1,), (1,)), ((), ())))
            score = jnp.where(causal, score, 0.0).astype(BF16)
            intra[block_rows(b), heads[h]] = dot(score, value)

    wait_all(infos.at[pl.ds(0, NZ - 1)], info_r)
    firsts = [infos[j, 0:1, :] for j in range(NZ)]
    lasts = [infos[j, 1:2, :] for j in range(NZ)]
    stays = [same(firsts[j], lasts[j]) for j in range(NZ)]
    follows = [None] + [same(firsts[j], lasts[j - 1]) for j in range(1, NZ)]
    for g in range(NG):
        wait_all(pieces.at[g, pl.ds(0, NZ - 1)], t_r.at[g])
        running = pieces[g, 0].astype(F32)
        for j in range(1, NZ):
            before = follows[j] * running
            ascan[g, j] = before
            running = pieces[g, j].astype(F32) + stays[j] * before
        rbuf[g, x, 0:PIECE, :] = running
        rbuf[g, x, PIECE:PIECE + 8, :] = jnp.broadcast_to(lasts[NZ - 1], (8, DH))
        for i in (2, 1, 3):
            remote(rbuf.at[g, x], rbuf.at[g, x], r_s, r_r.at[g], at_x(i)).start()
    for g in range(NG):
        wait_all(rbuf.at[g, pl.ds(0, NX - 1)], r_r.at[g])
        for j in range(NZ):
            into = ascan[g, j] if j > 0 else jnp.zeros((PIECE, DH), F32)
            for xx in range(NX - 1):
                hit = same(rbuf[g, xx, PIECE:PIECE + 1, :], firsts[j]) * jnp.where(xx < x, 1.0, 0.0)
                into = into + hit * rbuf[g, xx, 0:PIECE, :]
            csend[g, j] = into.astype(BF16)
        for i in far_first:
            remote(csend.at[g, (z + i) % NZ], carry.at[g, z], c_s, c_r.at[g], at_z(i)).start()
        carry[g, z] = csend[g, z]

    def w_ref(part, column, side):
        return wbuf.at[pl.ds(2 * part, 2), column, side]

    def w_copy(direction, step, part):
        source = (z - step) % NZ if direction == 0 else (z + step) % NZ
        ref = w_ref(part, source, core)
        to = at_z(1) if direction == 0 else at_z(NZ - 1)
        return remote(ref, ref, wz_s, wz_r.at[direction, step, part], to)

    def w_pair(ref):
        return remote(ref, ref, pair_s, pair_r, sibling)

    wait_all(wbuf.at[pl.ds(0, NX - 1), z, core], wx_r)
    for part in range(2):
        for direction in range(2):
            w_copy(direction, 0, part).start()
    w_pair(wbuf.at[:, z, core]).start()

    def w_arrive(step, part):
        for direction in range(2):
            if hops(direction, 2 * part) > step:
                w_copy(direction, step, part).wait_recv()
                if hops(direction, 2 * part) > step + 1:
                    w_copy(direction, step + 1, part).start()
                source = (z - 1 - step) % NZ if direction == 0 else (z + 1 + step) % NZ
                w_pair(w_ref(part, source, core)).start()

    def y_copy(direction, step, g, b):
        source = (tp - step) % NY if direction == 0 else (tp + step) % NY
        ref = feats.at[source, g, block_rows(b)]
        to = at_y(1) if direction == 0 else at_y(NY - 1)
        return remote(ref, ref, y_s, y_r.at[direction, step, g, b], to)

    def y_arrive(step, g, b):
        for direction in range(2):
            if hops(direction, b) > step:
                y_copy(direction, step, g, b).wait_recv()
                if hops(direction, b) > step + 1:
                    y_copy(direction, step + 1, g, b).start()

    loads[6].wait()
    gains = gain_ref[...]
    for g in range(NG):
        wait_all(carry.at[g, pl.ds(0, NZ - 1)], c_r.at[g])
        for b in range(NB):
            carried = same(segs[b], segs[0])
            for h in range(GH):
                head = g * GH + h
                state = carry[g, pl.ds(h * NZ // GH, NZ // GH)].reshape(DH, DH).astype(F32) * carried
                if b > 0:
                    state = state + local[b - 1, head]
                query = qbuf[ids[b], :, heads[head]]
                attended = intra[block_rows(b), heads[head]] + dot(query, state.astype(BF16))
                scale = lax.rsqrt(jnp.mean(attended * attended, axis=-1, keepdims=True) + 1e-06)
                normed = attended * scale * gains[:, head * DH:(head + 1) * DH]
                feats[tp, g, block_rows(b), heads[h]] = normed.astype(BF16)
            for direction in range(2):
                y_copy(direction, 0, g, b).start()

    def weights(source, g):
        return wbuf[source // 2, pl.ds(source % 2 * NH + g * GH, GH)].reshape(GC, NH * DH)

    def product(step):
        source = (tp + step) % NY
        total = dot(feats[source, 0], weights(source, 0)) + dot(feats[source, 1], weights(source, 1))
        acc[...] = total if step == 0 else acc[...] + total

    parts = [(g, b) for g in range(NG) for b in range(NB)]
    w_order = [(step, part) for step in range(4) for part in range(2)]
    for step in range(2):
        for i, (g, b) in enumerate(parts):
            y_arrive(step, g, b)
            if i % 2 == 1:
                w_arrive(*w_order[step * NB + i // 2])
    wait_all(wbuf.at[:, :, 1 - core], pair_r)
    for i, (g, b) in enumerate(parts):
        y_arrive(2, g, b)
        if i < 5:
            product((0, 1, NY - 1, 2, NY - 2)[i])
    product(3)
    product(NY - 3)

    far = (tp + NY // 2) % NY
    for g in range(NG):
        for b in (0, NB // 2, 1, NB // 2 + 1):
            y_arrive(3, g, b)
            rows = block_rows(b)
            total = acc[rows, :] + dot(feats[far, g, rows, :], weights(far, g))
            if g < NG - 1:
                acc[rows, :] = total
            else:
                out_ref[rows, :] = total.astype(BF16)

    wait_all(infos.at[pl.ds(0, NZ - 1)], info_s)
    wait_all(pieces.at[:, pl.ds(0, NZ - 1)], t_s)
    wait_all(rbuf.at[:, pl.ds(0, NX - 1)], r_s)
    wait_all(carry.at[:, pl.ds(0, NZ - 1)], c_s)
    wait_all(wbuf.at[pl.ds(0, NX - 1), z, core], wx_s)
    wait_all(wbuf.at[:, pl.ds(0, NZ - 1), core], wz_s)
    wait_all(wbuf.at[:, :, core], pair_s)
    wait_all(feats.at[pl.ds(0, NY - 1)], y_s)


def body(qkv_bank, pack_rows, segment, norm_gain, out_weight):
    rows, _, columns = qkv_bank.shape
    planes = jnp.transpose(qkv_bank, (1, 0, 2)).reshape(3, NB, BLK, columns)
    dma = pltpu.SemaphoreType.DMA
    return pl.pallas_call(
        kernel,
        out_shape=jax.ShapeDtypeStruct((rows, columns), BF16),
        in_specs=[pl.BlockSpec(memory_space=pl.ANY)] * 5,
        out_specs=pl.BlockSpec(memory_space=pltpu.VMEM),
        scratch_shapes=[
            pltpu.SMEM((NB,), jnp.int32),
            pltpu.SMEM((NB,), jnp.int32),
            pltpu.VMEM((1, columns), F32),
            pltpu.VMEM((NB, BLK, columns), BF16),
            pltpu.VMEM((NB, BLK, columns), BF16),
            pltpu.VMEM((NB, BLK, columns), BF16),
            pltpu.VMEM((NX, NZ, 2, HALF, columns), BF16),
            pltpu.VMEM((NY, NG, rows, GC), BF16),
            pltpu.VMEM((rows, columns), F32),
            pltpu.VMEM((rows, columns), F32),
            pltpu.VMEM((NB - 1, NH, DH, DH), F32),
            pltpu.VMEM((NG, GC, DH), BF16),
            pltpu.VMEM((NG, NZ, PIECE, DH), BF16),
            pltpu.VMEM((NZ, 2, DH), F32),
            pltpu.VMEM((NG, NZ, PIECE, DH), F32),
            pltpu.VMEM((NG, NX, PIECE + 8, DH), F32),
            pltpu.VMEM((NG, NZ, PIECE, DH), BF16),
            pltpu.VMEM((NG, NZ, PIECE, DH), BF16),
            dma((7,)), dma, dma, dma, dma((NG,)), dma, dma((NG,)), dma, dma((NG,)),
            dma, dma((2, 4, NG, NB)), dma, dma, dma, dma((2, 4, 2)), dma, dma,
        ],
        compiler_params=pltpu.CompilerParams(
            collective_id=0, has_side_effects=True, vmem_limit_bytes=60 * 1024 * 1024
        ),
    )(pack_rows, segment, planes, norm_gain.reshape(1, columns), out_weight.reshape(2, HALF, columns))


def solution(mesh):
    in_specs = (
        P(("dp", "seq"), None, "tp"),
        P(("dp", "seq")),
        P(("dp", "seq")),
        P("tp"),
        P("seq", "tp"),
    )
    out_specs = P(("dp", "seq"), "tp")
    return jax.shard_map(body, mesh=mesh, in_specs=in_specs, out_specs=out_specs, check_vma=False)
```

```python
import jax
import jax.numpy as jnp
from jax import lax
from jax.experimental import pallas as pl
from jax.experimental.pallas import tpu as pltpu
from jax.sharding import PartitionSpec as P

DH = 128
BLK = 128
NB = 4
NH = 4
NG = 2
GH = NH // NG
GC = GH * DH
NX, NZ, NY = 4, 8, 8
PIECE = GC // NZ
HALF = BLK // 2
MESH = pl.DeviceIdType.MESH
F32, BF16 = jnp.float32, jnp.bfloat16


def dot(a, b, dims=(((1,), (0,)), ((), ()))):
    return lax.dot_general(a, b, dims, preferred_element_type=F32)


def same(a, b):
    return jnp.maximum(1 - jnp.abs(a - b), 0).astype(F32)


def hops(direction, part):
    return 4 if (part < 2) == (direction == 0) else 3


def kernel(
    pack_hbm, seg_hbm, qkv_hbm, gain_hbm, w_hbm, out_hbm,
    pack_ref, seg_ref, gain_ref, qbuf, kbuf, vbuf, wbuf, feats, acc, intra, local, tsend, pieces, infos, ascan, rbuf,
    csend, carry, mixed,
    load_sem, out_sem, info_s, info_r, t_s, t_r, r_s, r_r, c_s, c_r,
    y_s, y_r0, y_r, wx_s, wx_r, wz_s, wz_r, pair_s, pair_r,
):
    seq, tp, core = lax.axis_index("seq"), lax.axis_index("tp"), lax.axis_index("dp")
    x, z = seq // NZ, seq % NZ

    def at_z(step):
        return {"seq": x * NZ + (z + step) % NZ, "tp": tp, "dp": core}

    def at_x(step):
        return {"seq": (x + step) % NX * NZ + z, "tp": tp, "dp": core}

    def at_y(step):
        return {"seq": seq, "tp": (tp + step) % NY, "dp": core}

    sibling = {"seq": seq, "tp": tp, "dp": 1 - core}

    def remote(src, dst, send, recv, device):
        return pltpu.make_async_remote_copy(
            src_ref=src, dst_ref=dst, send_sem=send, recv_sem=recv,
            device_id=device, device_id_type=MESH,
        )

    def wait_all(ref, sem):
        pltpu.make_async_copy(ref, ref, sem).wait()

    loads = [
        pltpu.make_async_copy(src, dst, load_sem.at[i])
        for i, (src, dst) in enumerate((
            (qkv_hbm.at[0], qbuf), (qkv_hbm.at[1], kbuf), (qkv_hbm.at[2], vbuf), (w_hbm.at[core], wbuf.at[x, z, core]),
            (pack_hbm, pack_ref), (seg_hbm, seg_ref), (gain_hbm, gain_ref),
        ))
    ]
    partners = [at_z(i) for i in (4, 3, 5, 2, 6, 1, 7)] + [at_x(i) for i in (2, 1, 3)]
    partners += [at_y(1), at_y(NY - 1), sibling]
    barrier = pltpu.get_barrier_semaphore()
    for device in partners:
        pl.semaphore_signal(barrier, inc=1, device_id=device, device_id_type=MESH)
    for i in (5, 4, 1, 2, 0, 3, 6):
        loads[i].start()
    loads[5].wait()
    loads[4].wait()
    segs = [seg_ref[b] for b in range(NB)]
    infos[z, 0:1, :] = jnp.broadcast_to(segs[0], (1, DH)).astype(F32)
    infos[z, 1:2, :] = jnp.broadcast_to(segs[NB - 1], (1, DH)).astype(F32)

    ids = [lax.rem(pack_ref[b], NB) for b in range(NB)]
    heads = [pl.ds(h * DH, DH) for h in range(NH)]
    joins = [None] + [same(segs[b], segs[b - 1]) for b in range(1, NB)]

    def update(g):
        for h in range(GH):
            head = g * GH + h
            total = None
            for b in range(NB):
                key = kbuf[ids[b], :, heads[head]]
                value = vbuf[ids[b], :, heads[head]]
                new = dot(key, value, (((0,), (0,)), ((), ())))
                if b > 0:
                    before = total * joins[b]
                    local[b - 1, head] = before
                    total = before + new
                else:
                    total = new
            tsend[g, pl.ds(h * DH, DH), :] = total.astype(BF16)
        pieces[g, z] = tsend[g, piece(z), :]

    def piece(j):
        return pl.ds(pl.multiple_of(j * PIECE, PIECE), PIECE)

    far_first = (4, 3, 5, 2, 6, 1, 7)
    def send_tails(g):
        for i in far_first:
            remote(tsend.at[g, piece((z + i) % NZ)], pieces.at[g, z], t_s, t_r.at[g], at_z(i)).start()

    loads[1].wait()
    loads[2].wait()
    update(0)
    update(1)
    pl.semaphore_wait(barrier, len(partners))
    for i in far_first:
        remote(infos.at[z], infos.at[z], info_s, info_r, at_z(i)).start()
    send_tails(0)
    send_tails(1)
    loads[3].wait()
    for i in (2, 1, 3):
        remote(wbuf.at[x, z, core], wbuf.at[x, z, core], wx_s, wx_r, at_x(i)).start()

    loads[0].wait()
    causal = lax.broadcasted_iota(jnp.int32, (BLK, BLK), 0) >= lax.broadcasted_iota(jnp.int32, (BLK, BLK), 1)

    def block_rows(b):
        return pl.ds(b * BLK, BLK)

    for h in range(NH):
        for b in range(NB):
            query = qbuf[ids[b], :, heads[h]]
            key = kbuf[ids[b], :, heads[h]]
            value = vbuf[ids[b], :, heads[h]]
            score = dot(query, key, (((1,), (1,)), ((), ())))
            score = jnp.where(causal, score, 0.0).astype(BF16)
            intra[block_rows(b), heads[h]] = dot(score, value)

    wait_all(infos.at[pl.ds(0, NZ - 1)], info_r)
    firsts = [infos[j, 0:1, :] for j in range(NZ)]
    lasts = [infos[j, 1:2, :] for j in range(NZ)]
    stays = [same(firsts[j], lasts[j]) for j in range(NZ)]
    follows = [None] + [same(firsts[j], lasts[j - 1]) for j in range(1, NZ)]
    for g in range(NG):
        wait_all(pieces.at[g, pl.ds(0, NZ - 1)], t_r.at[g])
        running = pieces[g, 0].astype(F32)
        for j in range(1, NZ):
            before = follows[j] * running
            ascan[g, j] = before
            running = pieces[g, j].astype(F32) + stays[j] * before
        rbuf[g, x, 0:PIECE, :] = running
        rbuf[g, x, PIECE:PIECE + 8, :] = jnp.broadcast_to(lasts[NZ - 1], (8, DH))
        for i in (2, 1, 3):
            remote(rbuf.at[g, x], rbuf.at[g, x], r_s, r_r.at[g], at_x(i)).start()
    for g in range(NG):
        wait_all(rbuf.at[g, pl.ds(0, NX - 1)], r_r.at[g])
        for j in range(NZ):
            into = ascan[g, j] if j > 0 else jnp.zeros((PIECE, DH), F32)
            for xx in range(NX - 1):
                hit = same(rbuf[g, xx, PIECE:PIECE + 1, :], firsts[j]) * jnp.where(xx < x, 1.0, 0.0)
                into = into + hit * rbuf[g, xx, 0:PIECE, :]
            csend[g, j] = into.astype(BF16)
        for i in far_first:
            remote(csend.at[g, (z + i) % NZ], carry.at[g, z], c_s, c_r.at[g], at_z(i)).start()
        carry[g, z] = csend[g, z]

    def w_ref(part, column, side):
        return wbuf.at[pl.ds(2 * part, 2), column, side]

    def w_copy(direction, step, part):
        source = (z - step) % NZ if direction == 0 else (z + step) % NZ
        ref = w_ref(part, source, core)
        to = at_z(1) if direction == 0 else at_z(NZ - 1)
        return remote(ref, ref, wz_s, wz_r.at[direction, step, part], to)

    def w_pair(ref):
        return remote(ref, ref, pair_s, pair_r, sibling)

    wait_all(wbuf.at[pl.ds(0, NX - 1), z, core], wx_r)
    for part in range(2):
        for direction in range(2):
            w_copy(direction, 0, part).start()
    w_pair(wbuf.at[:, z, core]).start()

    def w_arrive(step, part):
        for direction in range(2):
            if hops(direction, 2 * part) > step:
                w_copy(direction, step, part).wait_recv()
                if hops(direction, 2 * part) > step + 1:
                    w_copy(direction, step + 1, part).start()
                source = (z - 1 - step) % NZ if direction == 0 else (z + 1 + step) % NZ
                w_pair(w_ref(part, source, core)).start()

    def y_own(direction, g, b):
        ref = feats.at[tp, g, block_rows(b)]
        return remote(ref, ref, y_s, y_r0.at[direction, g, b], at_y(1) if direction == 0 else at_y(NY - 1))

    def y_copy(direction, step, b):
        source = (tp - step) % NY if direction == 0 else (tp + step) % NY
        ref = feats.at[source, :, block_rows(b)]
        to = at_y(1) if direction == 0 else at_y(NY - 1)
        return remote(ref, ref, y_s, y_r.at[direction, step - 1, b], to)

    def y_arrive(step, i):
        for direction in range(2):
            b = y_order[direction][i]
            if hops(direction, b) > step:
                if step == 0:
                    for g in range(NG):
                        y_own(direction, g, b).wait_recv()
                else:
                    y_copy(direction, step, b).wait_recv()
                if hops(direction, b) > step + 1:
                    y_copy(direction, step + 1, b).start()

    y_order = ((0, 1, 2, 3), (2, 3, 0, 1))
    ready = {0: ((0, 0),), 2: ((1, 2),), 1: ((0, 1), (0, 2)), 3: ((1, 3), (1, 0), (1, 1), (0, 3))}
    loads[6].wait()
    gains = gain_ref[...]
    for g in range(NG):
        wait_all(carry.at[g, pl.ds(0, NZ - 1)], c_r.at[g])
        for b in (0, 2, 1, 3):
            carried = same(segs[b], segs[0])
            for h in range(GH):
                head = g * GH + h
                state = carry[g, pl.ds(h * NZ // GH, NZ // GH)].reshape(DH, DH).astype(F32) * carried
                if b > 0:
                    state = state + local[b - 1, head]
                query = qbuf[ids[b], :, heads[head]]
                attended = intra[block_rows(b), heads[head]] + dot(query, state.astype(BF16))
                scale = lax.rsqrt(jnp.mean(attended * attended, axis=-1, keepdims=True) + 1e-06)
                normed = attended * scale * gains[:, head * DH:(head + 1) * DH]
                feats[tp, g, block_rows(b), heads[h]] = normed.astype(BF16)
            for direction, part in ready[b]:
                y_own(direction, g, part).start()

    def weights(source, g):
        return wbuf[source // 2, pl.ds(source % 2 * NH + g * GH, GH)].reshape(GC, NH * DH)

    def product(step):
        source = (tp + step) % NY
        total = dot(feats[source, 0], weights(source, 0)) + dot(feats[source, 1], weights(source, 1))
        acc[...] = total if step == 0 else acc[...] + total

    w_order = [(step, part) for step in range(4) for part in range(2)]
    for step in range(2):
        for i in range(NB):
            y_arrive(step, i)
            w_arrive(*w_order[step * NB + i])
    wait_all(wbuf.at[:, :, 1 - core], pair_r)
    for i in range(NB):
        y_arrive(2, i)
        product((0, 1, NY - 1, 2)[i])
    product(NY - 2)
    product(3)
    product(NY - 3)

    far = (tp + NY // 2) % NY
    for i in range(NB // 2):
        y_arrive(3, i)
        for b in (i, i + NB // 2):
            rows = block_rows(b)
            total = acc[rows, :]
            for g in range(NG):
                total = total + dot(feats[far, g, rows, :], weights(far, g))
            mixed[rows, :] = total.astype(BF16)
            pltpu.make_async_copy(mixed.at[rows], out_hbm.at[rows], out_sem).start()

    wait_all(infos.at[pl.ds(0, NZ - 1)], info_s)
    wait_all(pieces.at[:, pl.ds(0, NZ - 1)], t_s)
    wait_all(rbuf.at[:, pl.ds(0, NX - 1)], r_s)
    wait_all(carry.at[:, pl.ds(0, NZ - 1)], c_s)
    wait_all(wbuf.at[pl.ds(0, NX - 1), z, core], wx_s)
    wait_all(wbuf.at[:, pl.ds(0, NZ - 1), core], wz_s)
    wait_all(wbuf.at[:, :, core], pair_s)
    wait_all(feats.at[pl.ds(0, NY - 1)], y_s)
    wait_all(mixed, out_sem)


def body(qkv_bank, pack_rows, segment, norm_gain, out_weight):
    rows, _, columns = qkv_bank.shape
    planes = jnp.transpose(qkv_bank, (1, 0, 2)).reshape(3, NB, BLK, columns)
    dma = pltpu.SemaphoreType.DMA
    return pl.pallas_call(
        kernel,
        out_shape=jax.ShapeDtypeStruct((rows, columns), BF16),
        in_specs=[pl.BlockSpec(memory_space=pl.ANY)] * 5,
        out_specs=pl.BlockSpec(memory_space=pl.ANY),
        scratch_shapes=[
            pltpu.SMEM((NB,), jnp.int32),
            pltpu.SMEM((NB,), jnp.int32),
            pltpu.VMEM((1, columns), F32),
            pltpu.VMEM((NB, BLK, columns), BF16),
            pltpu.VMEM((NB, BLK, columns), BF16),
            pltpu.VMEM((NB, BLK, columns), BF16),
            pltpu.VMEM((NX, NZ, 2, HALF, columns), BF16),
            pltpu.VMEM((NY, NG, rows, GC), BF16),
            pltpu.VMEM((rows, columns), F32),
            pltpu.VMEM((rows, columns), F32),
            pltpu.VMEM((NB - 1, NH, DH, DH), F32),
            pltpu.VMEM((NG, GC, DH), BF16),
            pltpu.VMEM((NG, NZ, PIECE, DH), BF16),
            pltpu.VMEM((NZ, 2, DH), F32),
            pltpu.VMEM((NG, NZ, PIECE, DH), F32),
            pltpu.VMEM((NG, NX, PIECE + 8, DH), F32),
            pltpu.VMEM((NG, NZ, PIECE, DH), BF16),
            pltpu.VMEM((NG, NZ, PIECE, DH), BF16),
            pltpu.VMEM((rows, columns), BF16),
            dma((7,)), dma, dma, dma, dma, dma((NG,)), dma, dma((NG,)), dma, dma((NG,)),
            dma, dma((2, NG, NB)), dma((2, 3, NB)), dma, dma, dma, dma((2, 4, 2)), dma, dma,
        ],
        compiler_params=pltpu.CompilerParams(
            collective_id=0, has_side_effects=True, vmem_limit_bytes=60 * 1024 * 1024
        ),
    )(pack_rows, segment, planes, norm_gain.reshape(1, columns), out_weight.reshape(2, HALF, columns))


def solution(mesh):
    in_specs = (
        P(("dp", "seq"), None, "tp"),
        P(("dp", "seq")),
        P(("dp", "seq")),
        P("tp"),
        P("seq", "tp"),
    )
    out_specs = P(("dp", "seq"), "tp")
    return jax.shard_map(body, mesh=mesh, in_specs=in_specs, out_specs=out_specs, check_vma=False)
```

```python
import jax
import jax.numpy as jnp
from jax import lax
from jax.experimental import pallas as pl
from jax.experimental.pallas import tpu as pltpu
from jax.sharding import PartitionSpec as P

DH = 128
BLK = 128
NB = 4
NH = 4
NG = 2
GH = NH // NG
GC = GH * DH
NX, NZ, NY = 4, 8, 8
PIECE = GC // NZ
HALF = BLK // 2
MESH = pl.DeviceIdType.MESH
F32, BF16 = jnp.float32, jnp.bfloat16


def dot(a, b, dims=(((1,), (0,)), ((), ()))):
    return lax.dot_general(a, b, dims, preferred_element_type=F32)


def same(a, b):
    return jnp.maximum(1 - jnp.abs(a - b), 0).astype(F32)


def hops(direction, part):
    return 4 if (part < 2) == (direction == 0) else 3


def kernel(
    pack_hbm, seg_hbm, qkv_hbm, gain_hbm, w_hbm, out_hbm,
    pack_ref, seg_ref, gain_ref, qbuf, kbuf, vbuf, wbuf, feats, acc, intra, local, tsend, pieces, infos, ascan, rbuf,
    csend, carry, mixed,
    load_sem, out_sem, info_s, info_r, t_s, t_r, r_s, r_r, c_s, c_r,
    y_s, y_r, wx_s, wx_r, wz_s, wz_r, pair_s, pair_r,
):
    seq, tp, core = lax.axis_index("seq"), lax.axis_index("tp"), lax.axis_index("dp")
    x, z = seq // NZ, seq % NZ

    def at_z(step):
        return {"seq": x * NZ + (z + step) % NZ, "tp": tp, "dp": core}

    def at_x(step):
        return {"seq": (x + step) % NX * NZ + z, "tp": tp, "dp": core}

    def at_y(step):
        return {"seq": seq, "tp": (tp + step) % NY, "dp": core}

    sibling = {"seq": seq, "tp": tp, "dp": 1 - core}

    def remote(src, dst, send, recv, device):
        return pltpu.make_async_remote_copy(
            src_ref=src, dst_ref=dst, send_sem=send, recv_sem=recv,
            device_id=device, device_id_type=MESH,
        )

    def wait_all(ref, sem):
        pltpu.make_async_copy(ref, ref, sem).wait()

    loads = [
        pltpu.make_async_copy(src, dst, load_sem.at[i])
        for i, (src, dst) in enumerate((
            (qkv_hbm.at[0], qbuf), (qkv_hbm.at[1], kbuf), (qkv_hbm.at[2], vbuf), (w_hbm.at[core], wbuf.at[x, z, core]),
            (pack_hbm, pack_ref), (seg_hbm, seg_ref), (gain_hbm, gain_ref),
        ))
    ]
    partners = [at_z(i) for i in (4, 3, 5, 2, 6, 1, 7)] + [at_x(i) for i in (2, 1, 3)]
    partners += [at_y(1), at_y(NY - 1), sibling]
    barrier = pltpu.get_barrier_semaphore()
    for device in partners:
        pl.semaphore_signal(barrier, inc=1, device_id=device, device_id_type=MESH)
    for i in (5, 4, 1, 2, 0, 3, 6):
        loads[i].start()
    loads[5].wait()
    loads[4].wait()
    segs = [seg_ref[b] for b in range(NB)]
    infos[z, 0:1, :] = jnp.broadcast_to(segs[0], (1, DH)).astype(F32)
    infos[z, 1:2, :] = jnp.broadcast_to(segs[NB - 1], (1, DH)).astype(F32)

    ids = [lax.rem(pack_ref[b], NB) for b in range(NB)]
    heads = [pl.ds(h * DH, DH) for h in range(NH)]
    joins = [None] + [same(segs[b], segs[b - 1]) for b in range(1, NB)]

    def update(g):
        for h in range(GH):
            head = g * GH + h
            total = None
            for b in range(NB):
                key = kbuf[ids[b], :, heads[head]]
                value = vbuf[ids[b], :, heads[head]]
                new = dot(key, value, (((0,), (0,)), ((), ())))
                if b > 0:
                    before = total * joins[b]
                    local[b - 1, head] = before
                    total = before + new
                else:
                    total = new
            tsend[g, pl.ds(h * DH, DH), :] = total.astype(BF16)
        pieces[g, z] = tsend[g, piece(z), :]

    def piece(j):
        return pl.ds(pl.multiple_of(j * PIECE, PIECE), PIECE)

    far_first = (4, 3, 5, 2, 6, 1, 7)
    def send_tails(g):
        for i in far_first:
            remote(tsend.at[g, piece((z + i) % NZ)], pieces.at[g, z], t_s, t_r.at[g], at_z(i)).start()

    loads[1].wait()
    loads[2].wait()
    update(0)
    update(1)
    pl.semaphore_wait(barrier, len(partners))
    for i in far_first:
        remote(infos.at[z], infos.at[z], info_s, info_r, at_z(i)).start()
    send_tails(0)
    send_tails(1)
    loads[3].wait()
    for i in (2, 1, 3):
        remote(wbuf.at[x, z, core], wbuf.at[x, z, core], wx_s, wx_r, at_x(i)).start()

    loads[0].wait()
    causal = lax.broadcasted_iota(jnp.int32, (BLK, BLK), 0) >= lax.broadcasted_iota(jnp.int32, (BLK, BLK), 1)

    def block_rows(b):
        return pl.ds(b * BLK, BLK)

    def scores(h):
        for b in range(NB):
            query = qbuf[ids[b], :, heads[h]]
            key = kbuf[ids[b], :, heads[h]]
            value = vbuf[ids[b], :, heads[h]]
            score = dot(query, key, (((1,), (1,)), ((), ())))
            score = jnp.where(causal, score, 0.0).astype(BF16)
            intra[block_rows(b), heads[h]] = dot(score, value)

    scores(0)
    scores(1)

    wait_all(infos.at[pl.ds(0, NZ - 1)], info_r)
    firsts = [infos[j, 0:1, :] for j in range(NZ)]
    lasts = [infos[j, 1:2, :] for j in range(NZ)]
    stays = [same(firsts[j], lasts[j]) for j in range(NZ)]
    follows = [None] + [same(firsts[j], lasts[j - 1]) for j in range(1, NZ)]
    for g in range(NG):
        wait_all(pieces.at[g, pl.ds(0, NZ - 1)], t_r.at[g])
        running = pieces[g, 0].astype(F32)
        ascan[g, 0] = jnp.zeros((PIECE, DH), F32)
        for j in range(1, NZ):
            before = follows[j] * running
            ascan[g, j] = before
            running = pieces[g, j].astype(F32) + stays[j] * before
        rbuf[g, x, 0:PIECE, :] = running
        rbuf[g, x, PIECE:PIECE + 8, :] = jnp.broadcast_to(lasts[NZ - 1], (8, DH))
        for i in (2, 1):
            remote(rbuf.at[g, x], rbuf.at[g, x], r_s, r_r.at[g], at_x(i)).start()
    scores(2)
    for g in range(NG):
        wait_all(rbuf.at[g, pl.ds(0, 2)], r_r.at[g])
        for i in far_first + (0,):
            j = (z + i) % NZ
            into = ascan[g, j]
            for back in (1, 2):
                xx = (x + NX - back) % NX
                hit = same(rbuf[g, xx, PIECE:PIECE + 1, :], infos[j, 0:1, :]) * jnp.where(x >= back, 1.0, 0.0)
                into = into + hit * rbuf[g, xx, 0:PIECE, :]
            csend[g, j] = into.astype(BF16)
            if i > 0:
                remote(csend.at[g, j], carry.at[g, z], c_s, c_r.at[g], at_z(i)).start()
        carry[g, z] = csend[g, z]

    scores(3)

    def w_ref(part, column, side):
        return wbuf.at[pl.ds(2 * part, 2), column, side]

    def w_copy(direction, step, part):
        source = (z - step) % NZ if direction == 0 else (z + step) % NZ
        ref = w_ref(part, source, core)
        to = at_z(1) if direction == 0 else at_z(NZ - 1)
        return remote(ref, ref, wz_s, wz_r.at[direction, step, part], to)

    def w_pair(ref):
        return remote(ref, ref, pair_s, pair_r, sibling)

    wait_all(wbuf.at[pl.ds(0, NX - 1), z, core], wx_r)
    for part in range(2):
        for direction in range(2):
            w_copy(direction, 0, part).start()
    w_pair(wbuf.at[:, z, core]).start()

    def w_arrive(step, part):
        for direction in range(2):
            if hops(direction, 2 * part) > step:
                w_copy(direction, step, part).wait_recv()
                if hops(direction, 2 * part) > step + 1:
                    w_copy(direction, step + 1, part).start()
                source = (z - 1 - step) % NZ if direction == 0 else (z + 1 + step) % NZ
                w_pair(w_ref(part, source, core)).start()

    def y_own(direction, g, b):
        ref = feats.at[tp, g, block_rows(b)]
        return remote(ref, ref, y_s, y_r.at[direction, 0, b], at_y(1) if direction == 0 else at_y(NY - 1))

    def y_copy(direction, step, b):
        source = (tp - step) % NY if direction == 0 else (tp + step) % NY
        ref = feats.at[source, :, block_rows(b)]
        to = at_y(1) if direction == 0 else at_y(NY - 1)
        return remote(ref, ref, y_s, y_r.at[direction, step, b], to)

    def y_arrive(step, i):
        for direction in range(2):
            b = y_order[direction][i]
            if hops(direction, b) > step:
                y_copy(direction, step, b).wait_recv()
                if hops(direction, b) > step + 1:
                    y_copy(direction, step + 1, b).start()

    y_order = ((0, 1, 2, 3), (2, 3, 0, 1))
    ready = {b: ((0, b), (1, b)) for b in range(NB)}
    loads[6].wait()
    gains = gain_ref[...]
    for g in range(NG):
        wait_all(carry.at[g, pl.ds(0, NZ - 1)], c_r.at[g])
        for b in (0, 1, 2, 3):
            carried = same(segs[b], segs[0])
            for h in range(GH):
                head = g * GH + h
                state = carry[g, pl.ds(h * NZ // GH, NZ // GH)].reshape(DH, DH).astype(F32) * carried
                if b > 0:
                    state = state + local[b - 1, head]
                query = qbuf[ids[b], :, heads[head]]
                attended = intra[block_rows(b), heads[head]] + dot(query, state.astype(BF16))
                scale = lax.rsqrt(jnp.mean(attended * attended, axis=-1, keepdims=True) + 1e-06)
                normed = attended * scale * gains[:, head * DH:(head + 1) * DH]
                feats[tp, g, block_rows(b), heads[h]] = normed.astype(BF16)
            for direction, part in ready[b]:
                y_own(direction, g, part).start()

    def weights(source, g):
        return wbuf[source // 2, pl.ds(source % 2 * NH + g * GH, GH)].reshape(GC, NH * DH)

    def product(step):
        source = (tp + step) % NY
        total = dot(feats[source, 0], weights(source, 0)) + dot(feats[source, 1], weights(source, 1))
        acc[...] = total if step == 0 else acc[...] + total

    w_order = [(step, part) for step in range(4) for part in range(2)]
    for step in range(2):
        for i in range(NB):
            y_arrive(step, i)
            w_arrive(*w_order[step * NB + i])
    wait_all(wbuf.at[:, :, 1 - core], pair_r)
    for i in range(NB):
        y_arrive(2, i)
        product((0, 1, NY - 1, 2)[i])
    product(NY - 2)
    product(3)
    product(NY - 3)

    far = (tp + NY // 2) % NY
    for i in range(NB // 2):
        y_arrive(3, i)
        for b in (i, i + NB // 2):
            rows = block_rows(b)
            total = acc[rows, :]
            for g in range(NG):
                total = total + dot(feats[far, g, rows, :], weights(far, g))
            mixed[rows, :] = total.astype(BF16)
            pltpu.make_async_copy(mixed.at[rows], out_hbm.at[rows], out_sem).start()

    wait_all(infos.at[pl.ds(0, NZ - 1)], info_s)
    wait_all(pieces.at[:, pl.ds(0, NZ - 1)], t_s)
    wait_all(rbuf.at[:, pl.ds(0, 2)], r_s)
    wait_all(carry.at[:, pl.ds(0, NZ - 1)], c_s)
    wait_all(wbuf.at[pl.ds(0, NX - 1), z, core], wx_s)
    wait_all(wbuf.at[:, pl.ds(0, NZ - 1), core], wz_s)
    wait_all(wbuf.at[:, :, core], pair_s)
    wait_all(feats.at[pl.ds(0, NY - 1)], y_s)
    wait_all(mixed, out_sem)


def body(qkv_bank, pack_rows, segment, norm_gain, out_weight):
    rows, _, columns = qkv_bank.shape
    planes = jnp.transpose(qkv_bank, (1, 0, 2)).reshape(3, NB, BLK, columns)
    dma = pltpu.SemaphoreType.DMA
    return pl.pallas_call(
        kernel,
        out_shape=jax.ShapeDtypeStruct((rows, columns), BF16),
        in_specs=[pl.BlockSpec(memory_space=pl.ANY)] * 5,
        out_specs=pl.BlockSpec(memory_space=pl.ANY),
        scratch_shapes=[
            pltpu.SMEM((NB,), jnp.int32),
            pltpu.SMEM((NB,), jnp.int32),
            pltpu.VMEM((1, columns), F32),
            pltpu.VMEM((NB, BLK, columns), BF16),
            pltpu.VMEM((NB, BLK, columns), BF16),
            pltpu.VMEM((NB, BLK, columns), BF16),
            pltpu.VMEM((NX, NZ, 2, HALF, columns), BF16),
            pltpu.VMEM((NY, NG, rows, GC), BF16),
            pltpu.VMEM((rows, columns), F32),
            pltpu.VMEM((rows, columns), F32),
            pltpu.VMEM((NB - 1, NH, DH, DH), F32),
            pltpu.VMEM((NG, GC, DH), BF16),
            pltpu.VMEM((NG, NZ, PIECE, DH), BF16),
            pltpu.VMEM((NZ, 2, DH), F32),
            pltpu.VMEM((NG, NZ, PIECE, DH), F32),
            pltpu.VMEM((NG, NX, PIECE + 8, DH), F32),
            pltpu.VMEM((NG, NZ, PIECE, DH), BF16),
            pltpu.VMEM((NG, NZ, PIECE, DH), BF16),
            pltpu.VMEM((rows, columns), BF16),
            dma((7,)), dma, dma, dma, dma, dma((NG,)), dma, dma((NG,)), dma, dma((NG,)),
            dma, dma((2, 4, NB)), dma, dma, dma, dma((2, 4, 2)), dma, dma,
        ],
        compiler_params=pltpu.CompilerParams(
            collective_id=0, has_side_effects=True, vmem_limit_bytes=60 * 1024 * 1024
        ),
    )(pack_rows, segment, planes, norm_gain.reshape(1, columns), out_weight.reshape(2, HALF, columns))


def solution(mesh):
    in_specs = (
        P(("dp", "seq"), None, "tp"),
        P(("dp", "seq")),
        P(("dp", "seq")),
        P("tp"),
        P("seq", "tp"),
    )
    out_specs = P(("dp", "seq"), "tp")
    return jax.shard_map(body, mesh=mesh, in_specs=in_specs, out_specs=out_specs, check_vma=False)
```

```python
import jax
import jax.numpy as jnp
from jax import lax
from jax.experimental import pallas as pl
from jax.experimental.pallas import tpu as pltpu
from jax.sharding import PartitionSpec as P

DH = 128
BLK = 128
NB = 4
NH = 4
NG = 2
GH = NH // NG
GC = GH * DH
NX, NZ, NY = 4, 8, 8
PIECE = GC // NZ
HALF = BLK // 2
MESH = pl.DeviceIdType.MESH
F32, BF16 = jnp.float32, jnp.bfloat16


def dot(a, b, dims=(((1,), (0,)), ((), ()))):
    return lax.dot_general(a, b, dims, preferred_element_type=F32)


def same(a, b):
    return jnp.maximum(1 - jnp.abs(a - b), 0).astype(F32)


def hops(direction, part):
    return 4 if (part < 2) == (direction == 0) else 3


def kernel(
    pack_hbm, seg_hbm, qkv_hbm, gain_hbm, w_hbm, out_hbm,
    pack_ref, seg_ref, gain_ref, qbuf, kbuf, vbuf, wbuf, feats, acc, intra, local, tsend, pieces, infos, ascan, rbuf,
    csend, carry, mixed,
    load_sem, out_sem, info_s, info_r, t_s, t_r, r_s, r_r, c_s, c_r,
    y_s, y_r, wx_s, wx_r, wz_s, wz_r, pair_s, pair_r,
):
    seq, tp, core = lax.axis_index("seq"), lax.axis_index("tp"), lax.axis_index("dp")
    x, z = seq // NZ, seq % NZ

    def at_z(step):
        return {"seq": x * NZ + (z + step) % NZ, "tp": tp, "dp": core}

    def at_x(step):
        return {"seq": (x + step) % NX * NZ + z, "tp": tp, "dp": core}

    def at_y(step):
        return {"seq": seq, "tp": (tp + step) % NY, "dp": core}

    sibling = {"seq": seq, "tp": tp, "dp": 1 - core}

    def remote(src, dst, send, recv, device):
        return pltpu.make_async_remote_copy(
            src_ref=src, dst_ref=dst, send_sem=send, recv_sem=recv,
            device_id=device, device_id_type=MESH,
        )

    def wait_all(ref, sem):
        pltpu.make_async_copy(ref, ref, sem).wait()

    loads = [
        pltpu.make_async_copy(src, dst, load_sem.at[i])
        for i, (src, dst) in enumerate((
            (qkv_hbm.at[0], qbuf), (qkv_hbm.at[1], kbuf), (qkv_hbm.at[2], vbuf), (w_hbm.at[core], wbuf.at[x, z, core]),
            (pack_hbm, pack_ref), (seg_hbm, seg_ref), (gain_hbm, gain_ref),
        ))
    ]
    partners = [at_z(i) for i in (4, 3, 5, 2, 6, 1, 7)] + [at_x(i) for i in (2, 1, 3)]
    partners += [at_y(1), at_y(NY - 1), sibling]
    barrier = pltpu.get_barrier_semaphore()
    for device in partners:
        pl.semaphore_signal(barrier, inc=1, device_id=device, device_id_type=MESH)
    for i in (5, 4, 1, 2, 0, 3, 6):
        loads[i].start()
    loads[5].wait()
    loads[4].wait()
    segs = [seg_ref[b] for b in range(NB)]
    infos[z, 0:1, :] = jnp.broadcast_to(segs[0], (1, DH)).astype(F32)
    infos[z, 1:2, :] = jnp.broadcast_to(segs[NB - 1], (1, DH)).astype(F32)

    ids = [lax.rem(pack_ref[b], NB) for b in range(NB)]
    heads = [pl.ds(h * DH, DH) for h in range(NH)]
    joins = [None] + [same(segs[b], segs[b - 1]) for b in range(1, NB)]

    def update(g):
        for h in range(GH):
            head = g * GH + h
            total = None
            for b in range(NB):
                key = kbuf[ids[b], :, heads[head]]
                value = vbuf[ids[b], :, heads[head]]
                new = dot(key, value, (((0,), (0,)), ((), ())))
                if b > 0:
                    before = total * joins[b]
                    local[b - 1, head] = before
                    total = before + new
                else:
                    total = new
            tsend[g, pl.ds(h * DH, DH), :] = total.astype(BF16)
        pieces[g, z] = tsend[g, piece(z), :]

    def piece(j):
        return pl.ds(pl.multiple_of(j * PIECE, PIECE), PIECE)

    far_first = (4, 3, 5, 2, 6, 1, 7)
    def send_tails(g):
        for i in far_first:
            remote(tsend.at[g, piece((z + i) % NZ)], pieces.at[g, z], t_s, t_r.at[g], at_z(i)).start()

    loads[1].wait()
    loads[2].wait()
    update(0)
    update(1)
    pl.semaphore_wait(barrier, len(partners))
    for i in far_first:
        remote(infos.at[z], infos.at[z], info_s, info_r, at_z(i)).start()
    send_tails(0)
    send_tails(1)
    loads[3].wait()
    for i in (2, 1, 3):
        remote(wbuf.at[x, z, core], wbuf.at[x, z, core], wx_s, wx_r, at_x(i)).start()

    loads[0].wait()
    causal = lax.broadcasted_iota(jnp.int32, (BLK, BLK), 0) >= lax.broadcasted_iota(jnp.int32, (BLK, BLK), 1)

    def block_rows(b):
        return pl.ds(b * BLK, BLK)

    def scores(h):
        for b in range(NB):
            query = qbuf[ids[b], :, heads[h]]
            key = kbuf[ids[b], :, heads[h]]
            value = vbuf[ids[b], :, heads[h]]
            score = dot(query, key, (((1,), (1,)), ((), ())))
            score = jnp.where(causal, score, 0.0).astype(BF16)
            intra[block_rows(b), heads[h]] = dot(score, value)

    scores(0)
    scores(1)

    wait_all(infos.at[pl.ds(0, NZ - 1)], info_r)
    firsts = [infos[j, 0:1, :] for j in range(NZ)]
    lasts = [infos[j, 1:2, :] for j in range(NZ)]
    stays = [same(firsts[j], lasts[j]) for j in range(NZ)]
    follows = [None] + [same(firsts[j], lasts[j - 1]) for j in range(1, NZ)]
    for g in range(NG):
        wait_all(pieces.at[g, pl.ds(0, NZ - 1)], t_r.at[g])
        running = pieces[g, 0].astype(F32)
        ascan[g, 0] = jnp.zeros((PIECE, DH), F32)
        for j in range(1, NZ):
            before = follows[j] * running
            ascan[g, j] = before
            running = pieces[g, j].astype(F32) + stays[j] * before
        rbuf[g, x, 0:PIECE, :] = running.astype(BF16)
        rbuf[g, x, PIECE:PIECE + 16, :] = jnp.broadcast_to(lasts[NZ - 1], (16, DH)).astype(BF16)
        for i in (2, 1):
            remote(rbuf.at[g, x], rbuf.at[g, x], r_s, r_r.at[g], at_x(i)).start()
    scores(2)
    for g in range(NG):
        wait_all(rbuf.at[g, pl.ds(0, 2)], r_r.at[g])
        earlier = []
        for back in (1, 2):
            xx = (x + NX - back) % NX
            total = rbuf[g, xx, 0:PIECE, :].astype(F32) * jnp.where(x >= back, 1.0, 0.0)
            earlier.append((total, rbuf[g, xx, PIECE:PIECE + 16, :].astype(F32)[0:1]))
        for i in far_first + (0,):
            j = (z + i) % NZ
            into = ascan[g, j]
            for total, last in earlier:
                into = into + same(last, infos[j, 0:1, :]) * total
            csend[g, j] = into.astype(BF16)
            if i > 0:
                remote(csend.at[g, j], carry.at[g, z], c_s, c_r.at[g], at_z(i)).start()
        carry[g, z] = csend[g, z]

    scores(3)

    def w_ref(part, column, side):
        return wbuf.at[pl.ds(2 * part, 2), column, side]

    def w_copy(direction, step, part):
        source = (z - step) % NZ if direction == 0 else (z + step) % NZ
        ref = w_ref(part, source, core)
        to = at_z(1) if direction == 0 else at_z(NZ - 1)
        return remote(ref, ref, wz_s, wz_r.at[direction, step, part], to)

    def w_pair(ref):
        return remote(ref, ref, pair_s, pair_r, sibling)

    wait_all(wbuf.at[pl.ds(0, NX - 1), z, core], wx_r)
    for part in range(2):
        for direction in range(2):
            w_copy(direction, 0, part).start()
    w_pair(wbuf.at[:, z, core]).start()

    def w_arrive(step, part):
        for direction in range(2):
            if hops(direction, 2 * part) > step:
                w_copy(direction, step, part).wait_recv()
                if hops(direction, 2 * part) > step + 1:
                    w_copy(direction, step + 1, part).start()
                source = (z - 1 - step) % NZ if direction == 0 else (z + 1 + step) % NZ
                w_pair(w_ref(part, source, core)).start()

    def y_own(direction, g, b):
        ref = feats.at[tp, g, block_rows(b)]
        return remote(ref, ref, y_s, y_r.at[direction, 0, b], at_y(1) if direction == 0 else at_y(NY - 1))

    def y_copy(direction, step, b):
        source = (tp - step) % NY if direction == 0 else (tp + step) % NY
        ref = feats.at[source, :, block_rows(b)]
        to = at_y(1) if direction == 0 else at_y(NY - 1)
        return remote(ref, ref, y_s, y_r.at[direction, step, b], to)

    def y_arrive(step, i):
        for direction in range(2):
            b = y_order[direction][i]
            if hops(direction, b) > step:
                y_copy(direction, step, b).wait_recv()
                if hops(direction, b) > step + 1:
                    y_copy(direction, step + 1, b).start()

    y_order = ((0, 1, 2, 3), (2, 3, 0, 1))
    ready = {b: ((0, b), (1, b)) for b in range(NB)}
    loads[6].wait()
    gains = gain_ref[...]
    for g in range(NG):
        wait_all(carry.at[g, pl.ds(0, NZ - 1)], c_r.at[g])
        for b in (0, 1, 2, 3):
            carried = same(segs[b], segs[0])
            for h in range(GH):
                head = g * GH + h
                state = carry[g, pl.ds(h * NZ // GH, NZ // GH)].reshape(DH, DH).astype(F32) * carried
                if b > 0:
                    state = state + local[b - 1, head]
                query = qbuf[ids[b], :, heads[head]]
                attended = intra[block_rows(b), heads[head]] + dot(query, state.astype(BF16))
                scale = lax.rsqrt(jnp.mean(attended * attended, axis=-1, keepdims=True) + 1e-06)
                normed = attended * scale * gains[:, head * DH:(head + 1) * DH]
                feats[tp, g, block_rows(b), heads[h]] = normed.astype(BF16)
            for direction, part in ready[b]:
                y_own(direction, g, part).start()

    def weights(source, g):
        return wbuf[source // 2, pl.ds(source % 2 * NH + g * GH, GH)].reshape(GC, NH * DH)

    def product(step):
        source = (tp + step) % NY
        total = dot(feats[source, 0], weights(source, 0)) + dot(feats[source, 1], weights(source, 1))
        acc[...] = total if step == 0 else acc[...] + total

    w_order = [(step, part) for step in range(4) for part in range(2)]
    for step in range(2):
        for i in range(NB):
            y_arrive(step, i)
            w_arrive(*w_order[step * NB + i])
    wait_all(wbuf.at[:, :, 1 - core], pair_r)
    for i in range(NB):
        y_arrive(2, i)
        product((0, 1, NY - 1, 2)[i])
    product(NY - 2)
    product(3)
    product(NY - 3)

    far = (tp + NY // 2) % NY
    for i in range(NB // 2):
        y_arrive(3, i)
        for b in (i, i + NB // 2):
            rows = block_rows(b)
            total = acc[rows, :]
            for g in range(NG):
                total = total + dot(feats[far, g, rows, :], weights(far, g))
            mixed[rows, :] = total.astype(BF16)
            pltpu.make_async_copy(mixed.at[rows], out_hbm.at[rows], out_sem).start()

    wait_all(infos.at[pl.ds(0, NZ - 1)], info_s)
    wait_all(pieces.at[:, pl.ds(0, NZ - 1)], t_s)
    wait_all(rbuf.at[:, pl.ds(0, 2)], r_s)
    wait_all(carry.at[:, pl.ds(0, NZ - 1)], c_s)
    wait_all(wbuf.at[pl.ds(0, NX - 1), z, core], wx_s)
    wait_all(wbuf.at[:, pl.ds(0, NZ - 1), core], wz_s)
    wait_all(wbuf.at[:, :, core], pair_s)
    wait_all(feats.at[pl.ds(0, NY - 1)], y_s)
    wait_all(mixed, out_sem)


def body(qkv_bank, pack_rows, segment, norm_gain, out_weight):
    rows, _, columns = qkv_bank.shape
    planes = jnp.transpose(qkv_bank, (1, 0, 2)).reshape(3, NB, BLK, columns)
    dma = pltpu.SemaphoreType.DMA
    return pl.pallas_call(
        kernel,
        out_shape=jax.ShapeDtypeStruct((rows, columns), BF16),
        in_specs=[pl.BlockSpec(memory_space=pl.ANY)] * 5,
        out_specs=pl.BlockSpec(memory_space=pl.ANY),
        scratch_shapes=[
            pltpu.SMEM((NB,), jnp.int32),
            pltpu.SMEM((NB,), jnp.int32),
            pltpu.VMEM((1, columns), F32),
            pltpu.VMEM((NB, BLK, columns), BF16),
            pltpu.VMEM((NB, BLK, columns), BF16),
            pltpu.VMEM((NB, BLK, columns), BF16),
            pltpu.VMEM((NX, NZ, 2, HALF, columns), BF16),
            pltpu.VMEM((NY, NG, rows, GC), BF16),
            pltpu.VMEM((rows, columns), F32),
            pltpu.VMEM((rows, columns), F32),
            pltpu.VMEM((NB - 1, NH, DH, DH), F32),
            pltpu.VMEM((NG, GC, DH), BF16),
            pltpu.VMEM((NG, NZ, PIECE, DH), BF16),
            pltpu.VMEM((NZ, 2, DH), F32),
            pltpu.VMEM((NG, NZ, PIECE, DH), F32),
            pltpu.VMEM((NG, NX, PIECE + 16, DH), BF16),
            pltpu.VMEM((NG, NZ, PIECE, DH), BF16),
            pltpu.VMEM((NG, NZ, PIECE, DH), BF16),
            pltpu.VMEM((rows, columns), BF16),
            dma((7,)), dma, dma, dma, dma, dma((NG,)), dma, dma((NG,)), dma, dma((NG,)),
            dma, dma((2, 4, NB)), dma, dma, dma, dma((2, 4, 2)), dma, dma,
        ],
        compiler_params=pltpu.CompilerParams(
            collective_id=0, has_side_effects=True, vmem_limit_bytes=60 * 1024 * 1024
        ),
    )(pack_rows, segment, planes, norm_gain.reshape(1, columns), out_weight.reshape(2, HALF, columns))


def solution(mesh):
    in_specs = (
        P(("dp", "seq"), None, "tp"),
        P(("dp", "seq")),
        P(("dp", "seq")),
        P("tp"),
        P("seq", "tp"),
    )
    out_specs = P(("dp", "seq"), "tp")
    return jax.shard_map(body, mesh=mesh, in_specs=in_specs, out_specs=out_specs, check_vma=False)
```

```python
import jax
import jax.numpy as jnp
from jax import lax
from jax.experimental import pallas as pl
from jax.experimental.pallas import tpu as pltpu
from jax.sharding import PartitionSpec as P

DH = 128
BLK = 128
NB = 4
NH = 4
NG = 2
GH = NH // NG
GC = GH * DH
NX, NZ, NY = 4, 8, 8
PIECE = GC // NZ
HALF = BLK // 2
MESH = pl.DeviceIdType.MESH
F32, BF16 = jnp.float32, jnp.bfloat16


def dot(a, b, dims=(((1,), (0,)), ((), ()))):
    return lax.dot_general(a, b, dims, preferred_element_type=F32)


def same(a, b):
    return jnp.maximum(1 - jnp.abs(a - b), 0).astype(F32)


def hops(direction, part):
    return 4 if (part < 2) == (direction == 0) else 3


def kernel(
    pack_hbm, seg_hbm, qkv_hbm, gain_hbm, w_hbm, out_hbm,
    pack_ref, seg_ref, gain_ref, qbuf, kbuf, vbuf, wbuf, feats, acc, intra, local, tsend, pieces, infos, ascan, rbuf,
    csend, carry, mixed,
    load_sem, out_sem, info_s, info_r, t_s, t_r, r_s, r_r, c_s, c_r,
    y_s, y_r, wx_s, wx_r, wz_s, wz_r, pair_s, pair_r,
):
    seq, tp, core = lax.axis_index("seq"), lax.axis_index("tp"), lax.axis_index("dp")
    x, z = seq // NZ, seq % NZ

    def at_z(step):
        return {"seq": x * NZ + (z + step) % NZ, "tp": tp, "dp": core}

    def at_x(step):
        return {"seq": (x + step) % NX * NZ + z, "tp": tp, "dp": core}

    def at_y(step):
        return {"seq": seq, "tp": (tp + step) % NY, "dp": core}

    sibling = {"seq": seq, "tp": tp, "dp": 1 - core}

    def remote(src, dst, send, recv, device):
        return pltpu.make_async_remote_copy(
            src_ref=src, dst_ref=dst, send_sem=send, recv_sem=recv,
            device_id=device, device_id_type=MESH,
        )

    def wait_all(ref, sem):
        pltpu.make_async_copy(ref, ref, sem).wait()

    loads = [
        pltpu.make_async_copy(src, dst, load_sem.at[i])
        for i, (src, dst) in enumerate((
            (qkv_hbm.at[0], qbuf), (qkv_hbm.at[1], kbuf), (qkv_hbm.at[2], vbuf), (w_hbm.at[core], wbuf.at[x, z, core]),
            (pack_hbm, pack_ref), (seg_hbm, seg_ref), (gain_hbm, gain_ref),
        ))
    ]
    partners = [at_z(i) for i in (4, 3, 5, 2, 6, 1, 7)] + [at_x(i) for i in (2, 1, 3)]
    partners += [at_y(1), at_y(NY - 1), sibling]
    barrier = pltpu.get_barrier_semaphore()
    for device in partners:
        pl.semaphore_signal(barrier, inc=1, device_id=device, device_id_type=MESH)
    for i in (5, 4, 1, 2, 0, 3, 6):
        loads[i].start()
    loads[5].wait()
    loads[4].wait()
    segs = [seg_ref[b] for b in range(NB)]
    infos[z, 0:1, :] = jnp.broadcast_to(segs[0], (1, DH)).astype(F32)
    infos[z, 1:2, :] = jnp.broadcast_to(segs[NB - 1], (1, DH)).astype(F32)

    ids = [lax.rem(pack_ref[b], NB) for b in range(NB)]
    heads = [pl.ds(h * DH, DH) for h in range(NH)]
    joins = [None] + [same(segs[b], segs[b - 1]) for b in range(1, NB)]

    def update(g):
        for h in range(GH):
            head = g * GH + h
            total = None
            for b in range(NB):
                key = kbuf[ids[b], :, heads[head]]
                value = vbuf[ids[b], :, heads[head]]
                new = dot(key, value, (((0,), (0,)), ((), ())))
                if b > 0:
                    before = total * joins[b]
                    local[b - 1, head] = before
                    total = before + new
                else:
                    total = new
            tsend[g, pl.ds(h * DH, DH), :] = total.astype(BF16)
        pieces[g, z] = tsend[g, piece(z), :]

    def piece(j):
        return pl.ds(pl.multiple_of(j * PIECE, PIECE), PIECE)

    far_first = (4, 3, 5, 2, 6, 1, 7)
    def send_tails(g):
        for i in far_first:
            remote(tsend.at[g, piece((z + i) % NZ)], pieces.at[g, z], t_s, t_r.at[g], at_z(i)).start()

    loads[1].wait()
    loads[2].wait()
    update(0)
    update(1)
    pl.semaphore_wait(barrier, len(partners))
    for i in far_first:
        remote(infos.at[z], infos.at[z], info_s, info_r, at_z(i)).start()
    send_tails(0)
    send_tails(1)
    loads[3].wait()
    for i in (2, 1, 3):
        remote(wbuf.at[x, z, core], wbuf.at[x, z, core], wx_s, wx_r, at_x(i)).start()

    loads[0].wait()
    causal = lax.broadcasted_iota(jnp.int32, (BLK, BLK), 0) >= lax.broadcasted_iota(jnp.int32, (BLK, BLK), 1)

    def block_rows(b):
        return pl.ds(b * BLK, BLK)

    def scores(h):
        for b in range(NB):
            query = qbuf[ids[b], :, heads[h]]
            key = kbuf[ids[b], :, heads[h]]
            value = vbuf[ids[b], :, heads[h]]
            score = dot(query, key, (((1,), (1,)), ((), ())))
            score = jnp.where(causal, score, 0.0).astype(BF16)
            intra[block_rows(b), heads[h]] = dot(score, value)

    scores(0)
    scores(1)

    wait_all(infos.at[pl.ds(0, NZ - 1)], info_r)
    firsts = [infos[j, 0:1, :] for j in range(NZ)]
    lasts = [infos[j, 1:2, :] for j in range(NZ)]
    stays = [same(firsts[j], lasts[j]) for j in range(NZ)]
    follows = [None] + [same(firsts[j], lasts[j - 1]) for j in range(1, NZ)]
    for g in range(NG):
        wait_all(pieces.at[g, pl.ds(0, NZ - 1)], t_r.at[g])
        running = pieces[g, 0].astype(F32)
        ascan[g, 0] = jnp.zeros((PIECE, DH), F32)
        for j in range(1, NZ):
            before = follows[j] * running
            ascan[g, j] = before
            running = pieces[g, j].astype(F32) + stays[j] * before
        rbuf[g, x, 0:PIECE, :] = running.astype(BF16)
        rbuf[g, x, PIECE:PIECE + 16, :] = jnp.broadcast_to(lasts[NZ - 1], (16, DH)).astype(BF16)
        for i in (2, 1):
            pl.when(x + i < NX)(remote(rbuf.at[g, x], rbuf.at[g, x], r_s, r_r.at[g], at_x(i)).start)
    scores(2)
    for g in range(NG):
        for count, here in ((1, x == 1), (2, x >= 2)):
            pl.when(here)(lambda: wait_all(rbuf.at[g, pl.ds(0, count)], r_r.at[g]))
        earlier = []
        for back in (1, 2):
            xx = jnp.where(x >= back, x - back, x)
            total = rbuf[g, xx, 0:PIECE, :].astype(F32) * jnp.where(x >= back, 1.0, 0.0)
            earlier.append((total, rbuf[g, xx, PIECE:PIECE + 16, :].astype(F32)[0:1]))
        for i in far_first + (0,):
            j = (z + i) % NZ
            into = ascan[g, j]
            for total, last in earlier:
                into = into + same(last, infos[j, 0:1, :]) * total
            csend[g, j] = into.astype(BF16)
            if i > 0:
                remote(csend.at[g, j], carry.at[g, z], c_s, c_r.at[g], at_z(i)).start()
        carry[g, z] = csend[g, z]

    scores(3)

    def w_ref(part, column, side):
        return wbuf.at[pl.ds(2 * part, 2), column, side]

    def w_copy(direction, step, part):
        source = (z - step) % NZ if direction == 0 else (z + step) % NZ
        ref = w_ref(part, source, core)
        to = at_z(1) if direction == 0 else at_z(NZ - 1)
        return remote(ref, ref, wz_s, wz_r.at[direction, step, part], to)

    def w_pair(ref):
        return remote(ref, ref, pair_s, pair_r, sibling)

    wait_all(wbuf.at[pl.ds(0, NX - 1), z, core], wx_r)
    for part in range(2):
        for direction in range(2):
            w_copy(direction, 0, part).start()
    w_pair(wbuf.at[:, z, core]).start()

    def w_arrive(step, part):
        for direction in range(2):
            if hops(direction, 2 * part) > step:
                w_copy(direction, step, part).wait_recv()
                if hops(direction, 2 * part) > step + 1:
                    w_copy(direction, step + 1, part).start()
                source = (z - 1 - step) % NZ if direction == 0 else (z + 1 + step) % NZ
                w_pair(w_ref(part, source, core)).start()

    def y_own(direction, g, b):
        ref = feats.at[tp, g, block_rows(b)]
        return remote(ref, ref, y_s, y_r.at[direction, 0, b], at_y(1) if direction == 0 else at_y(NY - 1))

    def y_copy(direction, step, b):
        source = (tp - step) % NY if direction == 0 else (tp + step) % NY
        ref = feats.at[source, :, block_rows(b)]
        to = at_y(1) if direction == 0 else at_y(NY - 1)
        return remote(ref, ref, y_s, y_r.at[direction, step, b], to)

    def y_arrive(step, i):
        for direction in range(2):
            b = y_order[direction][i]
            if hops(direction, b) > step:
                y_copy(direction, step, b).wait_recv()
                if hops(direction, b) > step + 1:
                    y_copy(direction, step + 1, b).start()

    y_order = ((0, 1, 2, 3), (2, 3, 0, 1))
    ready = {b: ((0, b), (1, b)) for b in range(NB)}
    loads[6].wait()
    gains = gain_ref[...]
    for g in range(NG):
        wait_all(carry.at[g, pl.ds(0, NZ - 1)], c_r.at[g])
        for b in (0, 1, 2, 3):
            carried = same(segs[b], segs[0])
            for h in range(GH):
                head = g * GH + h
                state = carry[g, pl.ds(h * NZ // GH, NZ // GH)].reshape(DH, DH).astype(F32) * carried
                if b > 0:
                    state = state + local[b - 1, head]
                query = qbuf[ids[b], :, heads[head]]
                attended = intra[block_rows(b), heads[head]] + dot(query, state.astype(BF16))
                scale = lax.rsqrt(jnp.mean(attended * attended, axis=-1, keepdims=True) + 1e-06)
                normed = attended * scale * gains[:, head * DH:(head + 1) * DH]
                feats[tp, g, block_rows(b), heads[h]] = normed.astype(BF16)
            for direction, part in ready[b]:
                y_own(direction, g, part).start()

    def weights(source, g):
        return wbuf[source // 2, pl.ds(source % 2 * NH + g * GH, GH)].reshape(GC, NH * DH)

    def product(step):
        source = (tp + step) % NY
        total = dot(feats[source, 0], weights(source, 0)) + dot(feats[source, 1], weights(source, 1))
        acc[...] = total if step == 0 else acc[...] + total

    w_order = [(step, part) for step in range(4) for part in range(2)]
    for step in range(2):
        for i in range(NB):
            y_arrive(step, i)
            w_arrive(*w_order[step * NB + i])
    wait_all(wbuf.at[:, :, 1 - core], pair_r)
    for i in range(NB):
        y_arrive(2, i)
        product((0, 1, NY - 1, 2)[i])
    product(NY - 2)
    product(3)
    product(NY - 3)

    far = (tp + NY // 2) % NY
    for i in range(NB // 2):
        y_arrive(3, i)
        for b in (i, i + NB // 2):
            rows = block_rows(b)
            total = acc[rows, :]
            for g in range(NG):
                total = total + dot(feats[far, g, rows, :], weights(far, g))
            mixed[rows, :] = total.astype(BF16)
            pltpu.make_async_copy(mixed.at[rows], out_hbm.at[rows], out_sem).start()

    wait_all(infos.at[pl.ds(0, NZ - 1)], info_s)
    wait_all(pieces.at[:, pl.ds(0, NZ - 1)], t_s)
    for count, here in ((2, x < NX - 2), (1, x == NX - 2)):
        pl.when(here)(lambda: wait_all(rbuf.at[:, pl.ds(0, count)], r_s))
    wait_all(carry.at[:, pl.ds(0, NZ - 1)], c_s)
    wait_all(wbuf.at[pl.ds(0, NX - 1), z, core], wx_s)
    wait_all(wbuf.at[:, pl.ds(0, NZ - 1), core], wz_s)
    wait_all(wbuf.at[:, :, core], pair_s)
    wait_all(feats.at[pl.ds(0, NY - 1)], y_s)
    wait_all(mixed, out_sem)


def body(qkv_bank, pack_rows, segment, norm_gain, out_weight):
    rows, _, columns = qkv_bank.shape
    planes = jnp.transpose(qkv_bank, (1, 0, 2)).reshape(3, NB, BLK, columns)
    dma = pltpu.SemaphoreType.DMA
    return pl.pallas_call(
        kernel,
        out_shape=jax.ShapeDtypeStruct((rows, columns), BF16),
        in_specs=[pl.BlockSpec(memory_space=pl.ANY)] * 5,
        out_specs=pl.BlockSpec(memory_space=pl.ANY),
        scratch_shapes=[
            pltpu.SMEM((NB,), jnp.int32),
            pltpu.SMEM((NB,), jnp.int32),
            pltpu.VMEM((1, columns), F32),
            pltpu.VMEM((NB, BLK, columns), BF16),
            pltpu.VMEM((NB, BLK, columns), BF16),
            pltpu.VMEM((NB, BLK, columns), BF16),
            pltpu.VMEM((NX, NZ, 2, HALF, columns), BF16),
            pltpu.VMEM((NY, NG, rows, GC), BF16),
            pltpu.VMEM((rows, columns), F32),
            pltpu.VMEM((rows, columns), F32),
            pltpu.VMEM((NB - 1, NH, DH, DH), F32),
            pltpu.VMEM((NG, GC, DH), BF16),
            pltpu.VMEM((NG, NZ, PIECE, DH), BF16),
            pltpu.VMEM((NZ, 2, DH), F32),
            pltpu.VMEM((NG, NZ, PIECE, DH), F32),
            pltpu.VMEM((NG, NX, PIECE + 16, DH), BF16),
            pltpu.VMEM((NG, NZ, PIECE, DH), BF16),
            pltpu.VMEM((NG, NZ, PIECE, DH), BF16),
            pltpu.VMEM((rows, columns), BF16),
            dma((7,)), dma, dma, dma, dma, dma((NG,)), dma, dma((NG,)), dma, dma((NG,)),
            dma, dma((2, 4, NB)), dma, dma, dma, dma((2, 4, 2)), dma, dma,
        ],
        compiler_params=pltpu.CompilerParams(
            collective_id=0, has_side_effects=True, vmem_limit_bytes=60 * 1024 * 1024
        ),
    )(pack_rows, segment, planes, norm_gain.reshape(1, columns), out_weight.reshape(2, HALF, columns))


def solution(mesh):
    in_specs = (
        P(("dp", "seq"), None, "tp"),
        P(("dp", "seq")),
        P(("dp", "seq")),
        P("tp"),
        P("seq", "tp"),
    )
    out_specs = P(("dp", "seq"), "tp")
    return jax.shard_map(body, mesh=mesh, in_specs=in_specs, out_specs=out_specs, check_vma=False)
```
